512 devices in a mesh: psg: 64 (over x, z, core), qry: 8 (over y).
Axes of the slice: x: 4, y: 8, z: 8, core: 2. Of those that a mesh axis runs over, the one named last changes fastest.
Arguments:
- queries: bfloat16 [2048, 4096], P('psg', 'qry'), may hold values from -6 to 6
- grad_out: bfloat16 [2048, 4096], P('psg', 'qry'), may hold values from -6 to 6
- attn_out: bfloat16 [2048, 4096], P('psg', 'qry'), may hold values from -6 to 6
- log_sum: float32 [32, 2048], P('qry', 'psg'), may hold values from 3 to 5
- keys: bfloat16 [32768, 1024], P('psg', 'qry'), may hold values from -6 to 6
- values: bfloat16 [32768, 1024], P('psg', 'qry'), may hold values from -6 to 6
- proj_weight: bfloat16 [4096, 4096], P('psg', 'qry'), may hold values from -0.09375 to 0.09375
- attend: int32 [8, 16], replicated, may hold values from 0 to 63, all different within a row; in each aligned block of 8 rows (0 to 7, 8 to 15, ...) at most 4 rows name the same one
- qlen: int32 [8], replicated, may hold values from 128 to 256, as said below
Outputs:
- grad_query: float32 [2048, 4096], P('psg', 'qry')
- grad_keys: float32 [32768, 1024], P('psg', 'qry')
- grad_values: float32 [32768, 1024], P('psg', 'qry')
- grad_hidden: float32 [2048, 4096], P('psg')
The draws below stay inside these ranges and needn't reach their ends.
Inputs may be any that keep to these rules, and one draw needn't show every extreme that they name: `attend`: each question names 16 different blocks; each block is named by at least one question and at most 4, and some block by exactly 4. `qlen`: each a multiple of 128; some question has 256 rows.
All inputs are finite; a program needn't handle non-finite values.
Results may differ from the reference program's by a relative error of at most 0.0049.
Values may be sent and summed in bfloat16 or wider, within the bound.
No kernel may reach another device: no remote copies, remote signals or barrier semaphores. Data moves between devices by JAX's collectives and lax.ppermute only.
A program may use at most 64 MiB of HBM per device.

```python
import math
import jax
import jax.numpy as jnp
import numpy as np
from jax import lax

D = 4096
ASKING_COUNT = 32
SHARED_KV_COUNT = 8
ATTN_WIDTH = 128
GROUP = 4
PASSAGE_SPAN = 512
PASSAGES = 64
TILE = 128
QTILES = 2
PADDED_ASK_LEN = 256
NQ = 8
QROWS = 2048
TOPB = 16
CAP = 4


def draw_qlen(key, part):
    key = jax.random.fold_in(key, 11)
    first_key, second_key = jax.random.split(key)
    tiles = jax.random.randint(first_key, (NQ,), 1, QTILES + 1)
    longest = jax.random.randint(second_key, (), 0, NQ)
    tiles = jnp.where(jnp.arange(NQ) == longest, QTILES, tiles)
    return (tiles * TILE).astype(jnp.int32)


def levels(key, shape, shards, least, high):
    factor_of, own = 1.0, jax.random.fold_in(key, 6)
    for dim, blocks in shards:
        draws = jnp.exp(jax.random.uniform(jax.random.fold_in(own, dim), (blocks,), jnp.float32, least / len(shards), high / len(shards)))
        factor_of = factor_of * jnp.repeat(draws, shape[dim] // blocks).reshape([-1 if axis == dim else 1 for axis in range(len(shape))])
    return factor_of


def deal_out(stream_key, own, number, rows, amount, top, bound, lean):
    sequence = jax.random.permutation(stream_key, amount)
    packed, common = portions_of(amount, rows * top, bound, lean, True), portions_of(amount, rows * top, bound, lean, False)
    places = jnp.arange(amount)

    def named(tallies, rotation):
        used = int((tallies > 0).sum())
        fixed = max(1, used // 4)
        shifted = fixed + (places - fixed + rotation * (used - fixed)) % max(1, amount - fixed)
        return jnp.zeros((amount,), jnp.int32).at[sequence[jnp.where(places < fixed, places, shifted)]].set(jnp.asarray(tallies, jnp.int32))

    tallies = jnp.where(number % 4 == 0, named(packed, number // 4), named(common, number - number // 4 - 1))
    mixed = jax.random.permutation(jax.random.fold_in(own, 3), amount)
    donor, taker = mixed[0:amount // 2 * 2:2], mixed[1:amount // 2 * 2:2]
    room = jnp.minimum(tallies[donor] - 1, bound - tallies[taker]) // 2
    room = jnp.where((donor == sequence[0]) | (taker == sequence[0]) | (tallies[taker] == 0), 0, jnp.maximum(room, 0))
    shifted = jax.random.randint(jax.random.fold_in(own, 4), (amount // 2,), 0, 1 << 20) % (room + 1)
    tallies = tallies.at[donor].add(-shifted).at[taker].add(shifted)
    items = jnp.searchsorted(jnp.cumsum(tallies), jnp.arange(rows * top), side="right").astype(jnp.int32)
    listing = items.reshape(top, rows).T
    listing = listing[jax.random.permutation(jax.random.fold_in(own, 1), rows)]
    rotation = jax.random.randint(jax.random.fold_in(own, 2), (rows, 1), 0, top)
    return jnp.take_along_axis(listing, (jnp.arange(top)[None, :] + rotation) % top, axis=1)


def portions_of(amount, total, most, skew, full):
    loads = [(1 << 20) // math.isqrt(grade ** skew) + 1 for grade in range(1, amount + 1)]
    largest = most if full else min(most, max(-(-total // amount), total * loads[0] // sum(loads)))
    least = 1 if total - largest >= amount - 1 else 0
    given, surplus = [largest] + [least] * (amount - 1), total - largest - least * (amount - 1)
    while surplus > 0:
        candidates = [i for i in range(1, amount) if given[i] < largest] or [i for i in range(1, amount) if given[i] < most]
        whole, remaining = sum([loads[i] for i in candidates]), surplus
        for i in candidates:
            addition = min(most - given[i], max(1, remaining * loads[i] // whole), surplus)
            given[i] = given[i] + addition
            surplus = surplus - addition
    return np.array(given)


def bell_draw(rng, dims, width, reach, pieces=(), kind=jnp.bfloat16):
    level = levels(rng, dims, pieces, -0.22, 0.18) if pieces else 1.0
    values = jax.random.normal(rng, dims, jnp.float32) * width * level
    return jnp.minimum(jnp.maximum(values, -reach), reach).astype(kind)


def setup_inputs(seed: int = 0) -> dict:
    key_list = jax.random.split(jax.random.key(seed), 10)
    queries = bell_draw(key_list[0], (QROWS, ASKING_COUNT * ATTN_WIDTH), 1.0, 6.0, ((0, 64), (1, 8)))
    grad_out = bell_draw(key_list[1], (QROWS, ASKING_COUNT * ATTN_WIDTH), 1.0, 6.0, ((0, 64), (1, 8)))
    attn_out = bell_draw(key_list[2], (QROWS, ASKING_COUNT * ATTN_WIDTH), 1.0, 6.0, ((0, 64), (1, 8)))
    log_sum = jnp.clip(3.0 + 2.0 * jax.random.uniform(key_list[3], (ASKING_COUNT, QROWS), jnp.float32) ** levels(key_list[3], (ASKING_COUNT, QROWS), ((0, 8), (1, 64)), -0.2, 0.2), 3.0, 5.0)
    keys = bell_draw(key_list[4], (PASSAGES * PASSAGE_SPAN, SHARED_KV_COUNT * ATTN_WIDTH), 1.0, 6.0, ((0, 64), (1, 8)))
    values = bell_draw(key_list[5], (PASSAGES * PASSAGE_SPAN, SHARED_KV_COUNT * ATTN_WIDTH), 1.0, 6.0, ((0, 64), (1, 8)))
    proj_weight = bell_draw(key_list[6], (D, ASKING_COUNT * ATTN_WIDTH), (ASKING_COUNT * ATTN_WIDTH) ** -0.5, 0.09375, ((0, 64), (1, 8)))
    attend_keys = jax.random.split(jax.random.fold_in(key_list[7], 1), NQ // NQ)
    attend_turns = jax.random.permutation(jax.random.fold_in(key_list[7], 3), NQ // NQ)
    attend = jax.vmap(lambda own, number: deal_out(jax.random.fold_in(key_list[7], 2), own, number, NQ, PASSAGES, TOPB, CAP, 2))(attend_keys, attend_turns).reshape((NQ, TOPB))
    qlen = draw_qlen(jax.random.fold_in(key_list[9], 71), 0)
    return {"queries": queries, "grad_out": grad_out, "attn_out": attn_out, "log_sum": log_sum, "keys": keys, "values": values, "proj_weight": proj_weight, "attend": attend, "qlen": qlen}


def row_delta(grad_out, attn_out):
    products = grad_out.astype(jnp.float32) * attn_out.astype(jnp.float32)
    return jnp.sum(products.reshape(products.shape[0], ASKING_COUNT, ATTN_WIDTH), axis=2).T


def reference(queries, grad_out, attn_out, log_sum, keys, values, proj_weight, attend, qlen):
    inverse_root_dimension = ATTN_WIDTH ** -0.5
    delta = row_delta(grad_out, attn_out)

    def visit(totals, pair_index):
        grad_q, grad_k, grad_v = totals
        question = pair_index // TOPB
        passage = attend[question, pair_index % TOPB]
        row_start = (question * PADDED_ASK_LEN).astype(jnp.int32)
        key_start = (passage * PASSAGE_SPAN).astype(jnp.int32)
        asking_matrix_tile = lax.dynamic_slice_in_dim(queries, row_start, PADDED_ASK_LEN, 0).astype(jnp.float32).reshape(PADDED_ASK_LEN, SHARED_KV_COUNT, GROUP, ATTN_WIDTH)
        output_gradient_rows = lax.dynamic_slice_in_dim(grad_out, row_start, PADDED_ASK_LEN, 0).astype(jnp.float32).reshape(PADDED_ASK_LEN, SHARED_KV_COUNT, GROUP, ATTN_WIDTH)
        passage_lookup_matrix = lax.dynamic_slice_in_dim(keys, key_start, PASSAGE_SPAN, 0).astype(jnp.float32).reshape(PASSAGE_SPAN, SHARED_KV_COUNT, ATTN_WIDTH)
        value_block_rows = lax.dynamic_slice_in_dim(values, key_start, PASSAGE_SPAN, 0).astype(jnp.float32).reshape(PASSAGE_SPAN, SHARED_KV_COUNT, ATTN_WIDTH)
        lse_rows = lax.dynamic_slice_in_dim(log_sum, row_start, PADDED_ASK_LEN, 1).reshape(SHARED_KV_COUNT, GROUP, PADDED_ASK_LEN)
        delta_rows = lax.dynamic_slice_in_dim(delta, row_start, PADDED_ASK_LEN, 1).reshape(SHARED_KV_COUNT, GROUP, PADDED_ASK_LEN)
        row_valid = (jnp.arange(PADDED_ASK_LEN) < qlen[question]).astype(jnp.float32)
        raw_attention_energies = jnp.einsum('dlyb,ilb->lydi', asking_matrix_tile, passage_lookup_matrix) * inverse_root_dimension
        probs = jnp.exp(raw_attention_energies - lse_rows[..., None]) * row_valid[None, None, :, None]
        probability_narrow = lax.optimization_barrier(probs.astype(jnp.bfloat16)).astype(jnp.float32)
        probability_gradient = jnp.einsum('dlyb,ilb->lydi', output_gradient_rows, value_block_rows)
        dscore = probs * (probability_gradient - delta_rows[..., None])
        energy_derivative_lowprec = lax.optimization_barrier(dscore.astype(jnp.bfloat16)).astype(jnp.float32)
        asking_partial_term = (jnp.einsum('ilgy,yiu->gilu', energy_derivative_lowprec, passage_lookup_matrix) * inverse_root_dimension).reshape(PADDED_ASK_LEN, ASKING_COUNT * ATTN_WIDTH)
        lookup_partial_term = (jnp.einsum('nwde,dnwj->enj', energy_derivative_lowprec, asking_matrix_tile) * inverse_root_dimension).reshape(PASSAGE_SPAN, SHARED_KV_COUNT * ATTN_WIDTH)
        value_contribution = jnp.einsum('nwde,dnwj->enj', probability_narrow, output_gradient_rows).reshape(PASSAGE_SPAN, SHARED_KV_COUNT * ATTN_WIDTH)
        grad_q = lax.dynamic_update_slice_in_dim(grad_q, lax.dynamic_slice_in_dim(grad_q, row_start, PADDED_ASK_LEN, 0) + asking_partial_term, row_start, 0)
        grad_k = lax.dynamic_update_slice_in_dim(grad_k, lax.dynamic_slice_in_dim(grad_k, key_start, PASSAGE_SPAN, 0) + lookup_partial_term, key_start, 0)
        grad_v = lax.dynamic_update_slice_in_dim(grad_v, lax.dynamic_slice_in_dim(grad_v, key_start, PASSAGE_SPAN, 0) + value_contribution, key_start, 0)
        return (grad_q, grad_k, grad_v), None

    start_totals = (jnp.zeros((QROWS, ASKING_COUNT * ATTN_WIDTH), jnp.float32),
                    jnp.zeros((PASSAGES * PASSAGE_SPAN, SHARED_KV_COUNT * ATTN_WIDTH), jnp.float32),
                    jnp.zeros((PASSAGES * PASSAGE_SPAN, SHARED_KV_COUNT * ATTN_WIDTH), jnp.float32))
    totals, unused = lax.scan(visit, start_totals, jnp.arange(NQ * TOPB, dtype=jnp.int32))
    grad_query, grad_keys, grad_values = totals
    grad_hidden = jnp.dot(grad_query.astype(jnp.bfloat16), proj_weight.T, preferred_element_type=jnp.float32)
    return grad_query, grad_keys, grad_values, grad_hidden
```

```python
import functools

import jax
import jax.numpy as jnp
from jax import lax
from jax.experimental import pallas as pl
from jax.experimental.pallas import tpu as pltpu
from jax.sharding import PartitionSpec as P

WIDTH = 128
GROUP = 4
ASK_LEN = 256
XS, ZS, CS = 4, 8, 2
LOG2E = 1.4426950408889634
FAR = 1.0e6


def index_of(x, z, c):
    return (x * ZS + z) * CS + c


Z_GROUPS = [[index_of(x, z, c) for z in range(ZS)] for x in range(XS) for c in range(CS)]
X_GROUPS = [[index_of(x, z, c) for x in range(XS)] for z in range(ZS) for c in range(CS)]
CORE_SWAP = [(i, i ^ 1) for i in range(XS * ZS * CS)]


def pieces(value):
    high = lax.reduce_precision(value, 8, 7)
    rest = value - high
    middle = lax.reduce_precision(rest, 8, 7)
    low = rest - middle
    return [part.astype(jnp.bfloat16) for part in (high, middle, low)]


def pack_rows(queries, grad_out, attn_out, log_sum, qlen, owner):
    rows = queries.shape[0]
    heads = log_sum.shape[0]
    products = grad_out.astype(jnp.float32) * attn_out.astype(jnp.float32)
    delta = jnp.sum(products.reshape(rows, heads, WIDTH), axis=2)
    first = owner * rows
    question = first // ASK_LEN
    place = first - question * ASK_LEN + jnp.arange(rows)
    live = place < qlen[question]
    shift = jnp.where(live[:, None], log_sum.T * (WIDTH**0.5), FAR)
    columns = pieces(shift) + pieces(delta)
    side = jnp.concatenate(columns, axis=1)
    side = jnp.pad(side, ((0, 0), (0, WIDTH - side.shape[1])))
    return jnp.concatenate([queries, grad_out, side], axis=1)


def visit_kernel(heads, span, attending, own_ref, other_ref, key_ref, value_ref, own_q, other_q, out_k, out_v):
    question = pl.program_id(0)
    scale = WIDTH**-0.5
    half = ASK_LEN // 2

    @pl.when(question == 0)
    def _():
        out_k[...] = jnp.zeros_like(out_k)
        out_v[...] = jnp.zeros_like(out_v)

    @pl.when(attending[question] == 0)
    def _():
        own_q[...] = jnp.zeros_like(own_q)
        other_q[...] = jnp.zeros_like(other_q)

    @pl.when(attending[question] != 0)
    def _():
        key = key_ref[...]
        value = value_ref[...]
        key_t = key.astype(jnp.float32).T.astype(jnp.bfloat16)
        columns = lax.broadcasted_iota(jnp.int32, (span, WIDTH), 1)
        grad_k = jnp.zeros((span, WIDTH), jnp.float32)
        grad_v = jnp.zeros((span, WIDTH), jnp.float32)

        def take(start):
            both = [
                ref[0, :, :, start : start + WIDTH].reshape(half, WIDTH) for ref in (own_ref, other_ref)
            ]
            return jnp.concatenate(both, axis=0)

        side = take(2 * heads * WIDTH)
        for head in range(heads):
            query = take(head * WIDTH)
            cotangent = take((heads + head) * WIDTH)
            for_shift = (columns < 3 * heads) & (columns % heads == head)
            for_delta = (columns >= 3 * heads) & (columns < 6 * heads) & (columns % heads == head)
            minus_s = jnp.where(for_shift, -1.0, 0.0).astype(jnp.bfloat16)
            minus_d = jnp.where(for_delta, -1.0, 0.0).astype(jnp.bfloat16)
            energy = lax.dot_general(
                jnp.concatenate([key, minus_s], axis=1),
                jnp.concatenate([query, side], axis=1),
                (((1,), (1,)), ((), ())),
                preferred_element_type=jnp.float32,
            )
            prob = jnp.exp2(energy * (scale * LOG2E))
            change = lax.dot_general(
                jnp.concatenate([value, minus_d], axis=1),
                jnp.concatenate([cotangent, side], axis=1),
                (((1,), (1,)), ((), ())),
                preferred_element_type=jnp.float32,
            )
            low_score = (prob * change).astype(jnp.bfloat16)
            low_prob = prob.astype(jnp.bfloat16)
            grad_k = grad_k + jnp.dot(low_score, query, preferred_element_type=jnp.float32)
            grad_v = grad_v + jnp.dot(low_prob, cotangent, preferred_element_type=jnp.float32)
            term = jnp.dot(key_t, low_score, preferred_element_type=jnp.float32).T * scale
            term = term.astype(jnp.bfloat16)
            place = slice(head * WIDTH, (head + 1) * WIDTH)
            own_q[0, :, :, place] = term[:half].reshape(own_q.shape[1], own_q.shape[2], WIDTH)
            other_q[0, :, :, place] = term[half:].reshape(own_q.shape[1], own_q.shape[2], WIDTH)
        out_k[...] += grad_k * scale
        out_v[...] += grad_v


def visits(attending, own, other, keys, values, heads):
    questions, chunks, rows, packed = own.shape
    span = keys.shape[0]
    columns = heads * WIDTH
    block = pl.BlockSpec((1, chunks, rows, packed), lambda n, a: (n, 0, 0, 0))
    whole = pl.BlockSpec((span, WIDTH), lambda n, a: (0, 0))
    term = pl.BlockSpec((1, chunks, rows, columns), lambda n, a: (n, 0, 0, 0))
    return pl.pallas_call(
        functools.partial(visit_kernel, heads, span),
        grid_spec=pltpu.PrefetchScalarGridSpec(
            num_scalar_prefetch=1,
            grid=(questions,),
            in_specs=[block, block, whole, whole],
            out_specs=[term, term, whole, whole],
        ),
        out_shape=[
            jax.ShapeDtypeStruct((questions, chunks, rows, columns), jnp.bfloat16),
            jax.ShapeDtypeStruct((questions, chunks, rows, columns), jnp.bfloat16),
            jax.ShapeDtypeStruct((span, WIDTH), jnp.float32),
            jax.ShapeDtypeStruct((span, WIDTH), jnp.float32),
        ],
        compiler_params=pltpu.CompilerParams(vmem_limit_bytes=40 * 2**20),
        cost_estimate=pl.CostEstimate(flops=6 * 10**9, bytes_accessed=10**7, transcendentals=2 * 10**6),
    )(attending, own, other, keys, values)


def hidden_kernel(query_ref, weight_ref, out_ref):
    out_ref[0] = lax.dot_general(
        query_ref[...], weight_ref[...], (((1,), (1,)), ((), ())), preferred_element_type=jnp.float32
    ).astype(out_ref.dtype)


def hidden_parts(query_low, weight, parts):
    rows, columns = query_low.shape
    wide = weight.shape[0] // parts
    return pl.pallas_call(
        hidden_kernel,
        grid=(parts,),
        in_specs=[
            pl.BlockSpec((rows, columns), lambda n: (0, 0)),
            pl.BlockSpec((wide, columns), lambda n: (n, 0)),
        ],
        out_specs=pl.BlockSpec((1, rows, wide), lambda n: (n, 0, 0)),
        out_shape=jax.ShapeDtypeStruct((parts, rows, wide), jnp.bfloat16),
        cost_estimate=pl.CostEstimate(flops=2 * rows * columns * weight.shape[0], bytes_accessed=5 * 10**6, transcendentals=0),
    )(query_low, weight)


def on_device(queries, grad_out, attn_out, log_sum, keys, values, proj_weight, attend, qlen):
    heads = log_sum.shape[0]
    rows, columns = queries.shape
    owner = lax.axis_index("psg")
    weight = lax.all_gather(proj_weight, "psg", axis=0, tiled=True)

    packed = pack_rows(queries, grad_out, attn_out, log_sum, qlen, owner)
    gathered = lax.all_gather(packed, "psg", axis=0, axis_index_groups=Z_GROUPS)
    gathered = lax.all_gather(gathered, "psg", axis=0, axis_index_groups=X_GROUPS)
    question_total = attend.shape[0]
    own = gathered.reshape(question_total, -1, rows, packed.shape[1])
    other = lax.ppermute(own, "psg", CORE_SWAP)

    attending = jnp.any(attend == owner, axis=1).astype(jnp.int32)
    own_q, other_q, grad_keys, grad_values = visits(attending, own, other, keys, values, heads)

    swapped = lax.ppermute(other_q, "psg", CORE_SWAP)
    pair = (own_q.astype(jnp.float32) + swapped.astype(jnp.float32)).astype(jnp.bfloat16)
    pair = pair.reshape(XS, ZS, rows, columns)
    pair = lax.all_to_all(pair, "psg", 0, 0, tiled=True, axis_index_groups=X_GROUPS)
    line = jnp.sum(pair.astype(jnp.float32), axis=0).astype(jnp.bfloat16)
    line = lax.all_to_all(line, "psg", 0, 0, tiled=True, axis_index_groups=Z_GROUPS)
    grad_query = jnp.sum(line.astype(jnp.float32), axis=0)
    query_low = grad_query.astype(jnp.bfloat16)

    parts = lax.axis_size("qry")
    terms = hidden_parts(query_low, weight, parts)
    terms = lax.all_to_all(terms, "qry", 0, 0, tiled=True)
    hidden = jnp.sum(terms.astype(jnp.float32), axis=0)
    grad_hidden = lax.all_gather(hidden, "qry", axis=1, tiled=True)
    return (grad_query, grad_keys, grad_values, grad_hidden)


def solution(mesh):
    in_specs = (
        P("psg", "qry"),
        P("psg", "qry"),
        P("psg", "qry"),
        P("qry", "psg"),
        P("psg", "qry"),
        P("psg", "qry"),
        P("psg", "qry"),
        P(),
        P(),
    )
    out_specs = (P("psg", "qry"), P("psg", "qry"), P("psg", "qry"), P("psg", None))
    return jax.shard_map(
        on_device, mesh=mesh, in_specs=in_specs, out_specs=out_specs, check_vma=False
    )
```

```python
import functools

import jax
import jax.numpy as jnp
from jax import lax
from jax.experimental import pallas as pl
from jax.experimental.pallas import tpu as pltpu
from jax.sharding import PartitionSpec as P

WIDTH = 128
GROUP = 4
ASK_LEN = 256
XS, ZS, CS = 4, 8, 2
LOG2E = 1.4426950408889634
FAR = 1.0e6
WIDE = 60 * 2**20


def index_of(x, z, c):
    return (x * ZS + z) * CS + c


Z_GROUPS = [[index_of(x, z, c) for z in range(ZS)] for x in range(XS) for c in range(CS)]
X_GROUPS = [[index_of(x, z, c) for x in range(XS)] for z in range(ZS) for c in range(CS)]
C_GROUPS = [[index_of(x, z, c) for c in range(CS)] for x in range(XS) for z in range(ZS)]


def spread(blocks, axis, groups):
    return lax.all_to_all(blocks, axis, 0, 0, tiled=True, axis_index_groups=groups)


def pack_kernel(heads, qlen_ref, query_in, grad_in, output_in, lse_in, out_ref, query_ref, grad_ref, output_ref, lse_ref, sems):
    copies = [
        pltpu.make_async_copy(source, target, sems.at[k])
        for k, (source, target) in enumerate(
            ((grad_in, grad_ref), (output_in, output_ref), (lse_in, lse_ref), (query_in, query_ref))
        )
    ]
    for copy in copies:
        copy.start()
    rows, columns = query_ref.shape
    shape = (rows, WIDTH)
    owner = lax.axis_index("psg")
    per_question = ASK_LEN // rows
    question = lax.div(owner, per_question)
    first = (owner - question * per_question) * rows
    column = lax.broadcasted_iota(jnp.int32, shape, 1)
    row = lax.broadcasted_iota(jnp.int32, shape, 0)
    live = first + row < qlen_ref[question]
    square = lax.broadcasted_iota(jnp.int32, (rows, rows), 0) == lax.broadcasted_iota(jnp.int32, (rows, rows), 1)
    value = jnp.zeros(shape, jnp.float32)
    for copy in copies:
        copy.wait()
    for head in range(heads):
        part = slice(head * WIDTH, (head + 1) * WIDTH)
        products = grad_ref[:, part].astype(jnp.float32) * output_ref[:, part].astype(jnp.float32)
        delta = jnp.sum(products, axis=1, keepdims=True)
        spread_lse = jnp.broadcast_to(lse_ref[head : head + 1, :], (rows, rows))
        shift = jnp.sum(jnp.where(square, spread_lse, 0.0), axis=1, keepdims=True) * (WIDTH**0.5)
        shift = jnp.where(live, shift, FAR)
        value = jnp.where(column % heads == head, jnp.where(column < 3 * heads, shift, delta), value)
    high = value.astype(jnp.bfloat16).astype(jnp.float32)
    middle = (value - high).astype(jnp.bfloat16).astype(jnp.float32)
    low = value - high - middle
    piece = (column // heads) % 3
    side = jnp.where(piece == 0, high, jnp.where(piece == 1, middle, low))
    side = jnp.where(column < 6 * heads, side, 0.0).astype(jnp.bfloat16)
    for copy in range(out_ref.shape[0]):
        out_ref[copy, :, :columns] = query_ref[...]
        out_ref[copy, :, columns : 2 * columns] = grad_ref[...]
        out_ref[copy, :, 2 * columns :] = side


def pack_rows(queries, grad_out, attn_out, log_sum, qlen, copies):
    rows, columns = queries.shape
    heads = log_sum.shape[0]
    anywhere = pl.BlockSpec(memory_space=pl.ANY)
    return pl.pallas_call(
        functools.partial(pack_kernel, heads),
        in_specs=[pl.BlockSpec(memory_space=pltpu.SMEM)] + [anywhere] * 4,
        out_specs=pl.BlockSpec(memory_space=pltpu.VMEM),
        out_shape=jax.ShapeDtypeStruct((copies, rows, 2 * columns + WIDTH), jnp.bfloat16),
        scratch_shapes=[
            pltpu.VMEM((rows, columns), jnp.bfloat16),
            pltpu.VMEM((rows, columns), jnp.bfloat16),
            pltpu.VMEM((rows, columns), jnp.bfloat16),
            pltpu.VMEM((heads, rows), jnp.float32),
            pltpu.SemaphoreType.DMA((4,)),
        ],
        compiler_params=pltpu.CompilerParams(vmem_limit_bytes=WIDE),
    )(qlen, queries, grad_out, attn_out, log_sum)


def select_kernel(attend_ref, rows_ref, out_ref, plan_ref, sems):
    questions, top = attend_ref.shape
    slots = out_ref.shape[1]
    owner = lax.axis_index("psg")
    core = lax.rem(owner, CS)
    copies = []
    for target in range(CS):
        block = owner - core + target
        count = jnp.int32(0)
        chosen = [jnp.int32(0)] * slots
        for question in range(questions):
            hit = jnp.int32(0)
            for place in range(top):
                hit = hit | (attend_ref[question, place] == block).astype(jnp.int32)
            chosen = [jnp.where((hit == 1) & (count == k), question, chosen[k]) for k in range(slots)]
            count = count + hit

            @pl.when(core == target)
            def _():
                plan_ref[0, question] = hit
                plan_ref[1, question] = jnp.clip(count - 1, 0, slots - 1)

        for slot in range(slots):
            copy = pltpu.make_async_copy(
                rows_ref.at[chosen[slot]], out_ref.at[target, slot], sems.at[target * slots + slot]
            )
            copy.start()
            copies.append(copy)
    for copy in copies:
        copy.wait()


def select(attend, rows, slots):
    return pl.pallas_call(
        select_kernel,
        in_specs=[pl.BlockSpec(memory_space=pltpu.SMEM), pl.BlockSpec(memory_space=pl.ANY)],
        out_specs=[pl.BlockSpec(memory_space=pl.ANY), pl.BlockSpec(memory_space=pltpu.SMEM)],
        out_shape=[
            jax.ShapeDtypeStruct((CS, slots, *rows.shape[1:]), rows.dtype),
            jax.ShapeDtypeStruct((2, attend.shape[0]), jnp.int32),
        ],
        scratch_shapes=[pltpu.SemaphoreType.DMA((CS * slots,))],
    )(attend, rows)


def visit_kernel(heads, span, plan, rows_ref, key_ref, value_ref, out_q, out_k, out_v):
    question = pl.program_id(0)
    scale = WIDTH**-0.5

    @pl.when(question == 0)
    def _():
        out_k[...] = jnp.zeros_like(out_k)
        out_v[...] = jnp.zeros_like(out_v)

    @pl.when(plan[0, question] == 0)
    def _():
        out_q[...] = jnp.zeros_like(out_q)

    @pl.when(plan[0, question] != 0)
    def _():
        key = key_ref[...]
        value = value_ref[...]
        key_t = key.astype(jnp.float32).T.astype(jnp.bfloat16)
        columns = lax.broadcasted_iota(jnp.int32, (span, WIDTH), 1)
        grad_k = jnp.zeros((span, WIDTH), jnp.float32)
        grad_v = jnp.zeros((span, WIDTH), jnp.float32)

        def take(start):
            return rows_ref[:, 0, :, :, start : start + WIDTH].reshape(ASK_LEN, WIDTH)

        side = take(2 * heads * WIDTH)
        for head in range(heads):
            query = take(head * WIDTH)
            cotangent = take((heads + head) * WIDTH)
            for_shift = (columns < 3 * heads) & (columns % heads == head)
            for_delta = (columns >= 3 * heads) & (columns < 6 * heads) & (columns % heads == head)
            minus_s = jnp.where(for_shift, -1.0, 0.0).astype(jnp.bfloat16)
            minus_d = jnp.where(for_delta, -1.0, 0.0).astype(jnp.bfloat16)
            energy = lax.dot_general(
                jnp.concatenate([key, minus_s], axis=1),
                jnp.concatenate([query, side], axis=1),
                (((1,), (1,)), ((), ())),
                preferred_element_type=jnp.float32,
            )
            prob = jnp.exp2(energy * (scale * LOG2E))
            change = lax.dot_general(
                jnp.concatenate([value, minus_d], axis=1),
                jnp.concatenate([cotangent, side], axis=1),
                (((1,), (1,)), ((), ())),
                preferred_element_type=jnp.float32,
            )
            low_score = (prob * change).astype(jnp.bfloat16)
            low_prob = prob.astype(jnp.bfloat16)
            grad_k = grad_k + jnp.dot(low_score, query, preferred_element_type=jnp.float32)
            grad_v = grad_v + jnp.dot(low_prob, cotangent, preferred_element_type=jnp.float32)
            term = jnp.dot(key_t, low_score, preferred_element_type=jnp.float32).T * scale
            term = term.astype(jnp.bfloat16)
            place = slice(head * WIDTH, (head + 1) * WIDTH)
            out_q[:, 0, :, :, place] = term.reshape(out_q.shape[0], out_q.shape[2], out_q.shape[3], WIDTH)
        out_k[...] += grad_k * scale
        out_v[...] += grad_v


def visits(plan, rows, keys, values, heads):
    cores, _, chunks, chunk, packed = rows.shape
    questions = plan.shape[1]
    span = keys.shape[0]
    columns = heads * WIDTH
    whole = pl.BlockSpec((span, WIDTH), lambda n, p: (0, 0))
    return pl.pallas_call(
        functools.partial(visit_kernel, heads, span),
        grid_spec=pltpu.PrefetchScalarGridSpec(
            num_scalar_prefetch=1,
            grid=(questions,),
            in_specs=[
                pl.BlockSpec((cores, 1, chunks, chunk, packed), lambda n, p: (0, p[1, n], 0, 0, 0)),
                whole,
                whole,
            ],
            out_specs=[
                pl.BlockSpec((cores, 1, chunks, chunk, columns), lambda n, p: (0, n, 0, 0, 0)),
                whole,
                whole,
            ],
        ),
        out_shape=[
            jax.ShapeDtypeStruct((cores, questions, chunks, chunk, columns), jnp.bfloat16),
            jax.ShapeDtypeStruct((span, WIDTH), jnp.float32),
            jax.ShapeDtypeStruct((span, WIDTH), jnp.float32),
        ],
        compiler_params=pltpu.CompilerParams(vmem_limit_bytes=40 * 2**20),
    )(plan, rows, keys, values)


def hidden_kernel(query_ref, weight_ref, out_ref):
    out_ref[0] = lax.dot_general(
        query_ref[...], weight_ref[...], (((1,), (1,)), ((), ())), preferred_element_type=jnp.float32
    ).astype(out_ref.dtype)


def hidden_parts(query_low, weight, parts):
    rows, columns = query_low.shape
    wide = weight.shape[0] // parts
    return pl.pallas_call(
        hidden_kernel,
        grid=(parts,),
        in_specs=[
            pl.BlockSpec((rows, columns), lambda n: (0, 0)),
            pl.BlockSpec((wide, columns), lambda n: (n, 0)),
        ],
        out_specs=pl.BlockSpec((1, rows, wide), lambda n: (n, 0, 0)),
        out_shape=jax.ShapeDtypeStruct((parts, rows, wide), jnp.bfloat16),
        compiler_params=pltpu.CompilerParams(vmem_limit_bytes=WIDE),
    )(query_low, weight)


def on_device(queries, grad_out, attn_out, log_sum, keys, values, proj_weight, attend, qlen):
    heads = log_sum.shape[0]
    rows, columns = queries.shape
    weight = lax.all_gather(proj_weight, "psg", axis=0, tiled=True)

    packed = pack_rows(queries, grad_out, attn_out, log_sum, qlen, ZS)
    line = spread(packed, "psg", Z_GROUPS)
    gathered = spread(jnp.broadcast_to(line[None], (XS, *line.shape)), "psg", X_GROUPS)
    question_total, top = attend.shape
    gathered = gathered.reshape(question_total, -1, rows, packed.shape[2])
    slots = min(question_total, 2 * question_total * top // (XS * ZS * CS))
    chosen, plan = select(attend, gathered, slots)
    chosen = spread(chosen, "psg", C_GROUPS)

    terms, grad_keys, grad_values = visits(plan, chosen, keys, values, heads)

    terms = spread(terms, "psg", C_GROUPS)
    pair = jnp.sum(terms.astype(jnp.float32), axis=0).astype(jnp.bfloat16)
    pair = spread(pair.reshape(XS, ZS, rows, columns), "psg", X_GROUPS)
    line = jnp.sum(pair.astype(jnp.float32), axis=0).astype(jnp.bfloat16)
    line, weight = lax.optimization_barrier((line, weight))
    line = spread(line, "psg", Z_GROUPS)
    grad_query = jnp.sum(line.astype(jnp.float32), axis=0)
    query_low = grad_query.astype(jnp.bfloat16)

    parts = lax.axis_size("qry")
    terms = hidden_parts(query_low, weight, parts)
    terms = spread(terms, "qry", None)
    hidden = jnp.sum(terms.astype(jnp.float32), axis=0)
    hidden = spread(jnp.broadcast_to(hidden[None], (parts, *hidden.shape)), "qry", None)
    grad_hidden = jnp.swapaxes(hidden, 0, 1).reshape(rows, -1)
    return (grad_query, grad_keys, grad_values, grad_hidden)


def solution(mesh):
    in_specs = (
        P("psg", "qry"),
        P("psg", "qry"),
        P("psg", "qry"),
        P("qry", "psg"),
        P("psg", "qry"),
        P("psg", "qry"),
        P("psg", "qry"),
        P(),
        P(),
    )
    out_specs = (P("psg", "qry"), P("psg", "qry"), P("psg", "qry"), P("psg", None))
    return jax.shard_map(
        on_device, mesh=mesh, in_specs=in_specs, out_specs=out_specs, check_vma=False
    )
```

```python
import functools

import jax
import jax.numpy as jnp
from jax import lax
from jax.experimental import pallas as pl
from jax.experimental.pallas import tpu as pltpu
from jax.sharding import PartitionSpec as P

WIDTH = 128
GROUP = 4
ASK_LEN = 256
XS, ZS, CS = 4, 8, 2
LOG2E = 1.4426950408889634
FAR = 1.0e6
WIDE = 63 * 2**20


def index_of(x, z, c):
    return (x * ZS + z) * CS + c


Z_GROUPS = [[index_of(x, z, c) for z in range(ZS)] for x in range(XS) for c in range(CS)]
X_GROUPS = [[index_of(x, z, c) for x in range(XS)] for z in range(ZS) for c in range(CS)]
C_GROUPS = [[index_of(x, z, c) for c in range(CS)] for x in range(XS) for z in range(ZS)]

CORE_GROUPS = [[index_of(x, z, c) for x in range(XS) for z in range(ZS)] for c in range(CS)]
CORE_SWAP = [(i, i ^ 1) for i in range(XS * ZS * CS)]


def spread(blocks, axis, groups):
    return lax.all_to_all(blocks, axis, 0, 0, tiled=True, axis_index_groups=groups)


def pack_kernel(heads, qlen_ref, query_in, grad_in, output_in, lse_in, out_ref, query_ref, grad_ref, output_ref, lse_ref, sems):
    copies = [
        pltpu.make_async_copy(source, target, sems.at[k])
        for k, (source, target) in enumerate(
            ((grad_in, grad_ref), (output_in, output_ref), (lse_in, lse_ref), (query_in, query_ref))
        )
    ]
    for copy in copies:
        copy.start()
    rows, columns = query_ref.shape
    shape = (rows, WIDTH)
    owner = lax.axis_index("psg")
    per_question = ASK_LEN // rows
    question = lax.div(owner, per_question)
    first = (owner - question * per_question) * rows
    column = lax.broadcasted_iota(jnp.int32, shape, 1)
    row = lax.broadcasted_iota(jnp.int32, shape, 0)
    live = first + row < qlen_ref[question]
    square = lax.broadcasted_iota(jnp.int32, (rows, rows), 0) == lax.broadcasted_iota(jnp.int32, (rows, rows), 1)
    value = jnp.zeros(shape, jnp.float32)
    for copy in copies:
        copy.wait()
    for head in range(heads):
        part = slice(head * WIDTH, (head + 1) * WIDTH)
        products = grad_ref[:, part].astype(jnp.float32) * output_ref[:, part].astype(jnp.float32)
        delta = jnp.sum(products, axis=1, keepdims=True)
        spread_lse = jnp.broadcast_to(lse_ref[head : head + 1, :], (rows, rows))
        shift = jnp.sum(jnp.where(square, spread_lse, 0.0), axis=1, keepdims=True) * (WIDTH**0.5)
        shift = jnp.where(live, shift, FAR)
        value = jnp.where(column % heads == head, jnp.where(column < 3 * heads, shift, delta), value)
    high = value.astype(jnp.bfloat16).astype(jnp.float32)
    middle = (value - high).astype(jnp.bfloat16).astype(jnp.float32)
    low = value - high - middle
    piece = (column // heads) % 3
    side = jnp.where(piece == 0, high, jnp.where(piece == 1, middle, low))
    side = jnp.where(column < 6 * heads, side, 0.0).astype(jnp.bfloat16)
    for copy in range(out_ref.shape[0]):
        out_ref[copy, :, :columns] = query_ref[...]
        out_ref[copy, :, columns : 2 * columns] = grad_ref[...]
        out_ref[copy, :, 2 * columns :] = side


def pack_rows(queries, grad_out, attn_out, log_sum, qlen, copies):
    rows, columns = queries.shape
    heads = log_sum.shape[0]
    anywhere = pl.BlockSpec(memory_space=pl.ANY)
    return pl.pallas_call(
        functools.partial(pack_kernel, heads),
        in_specs=[pl.BlockSpec(memory_space=pltpu.SMEM)] + [anywhere] * 4,
        out_specs=pl.BlockSpec(memory_space=pltpu.VMEM),
        out_shape=jax.ShapeDtypeStruct((copies, rows, 2 * columns + WIDTH), jnp.bfloat16),
        scratch_shapes=[
            pltpu.VMEM((rows, columns), jnp.bfloat16),
            pltpu.VMEM((rows, columns), jnp.bfloat16),
            pltpu.VMEM((rows, columns), jnp.bfloat16),
            pltpu.VMEM((heads, rows), jnp.float32),
            pltpu.SemaphoreType.DMA((4,)),
        ],
        compiler_params=pltpu.CompilerParams(vmem_limit_bytes=WIDE),
    )(qlen, queries, grad_out, attn_out, log_sum)


def select_kernel(attend_ref, rows_ref, out_ref, plan_ref):
    questions, top = attend_ref.shape
    slots = out_ref.shape[1]
    owner = lax.axis_index("psg")
    core = lax.rem(owner, CS)
    for target in range(CS):
        block = owner - core + target
        count = jnp.int32(0)
        chosen = [jnp.int32(0)] * slots
        for question in range(questions):
            hit = jnp.int32(0)
            for place in range(top):
                hit = hit | (attend_ref[question, place] == block).astype(jnp.int32)
            chosen = [jnp.where((hit == 1) & (count == k), question, chosen[k]) for k in range(slots)]
            count = count + hit

            @pl.when(core == target)
            def _():
                plan_ref[0, question] = hit
                plan_ref[1, question] = jnp.clip(count - 1, 0, slots - 1)

        for slot in range(slots):
            out_ref[target, slot] = rows_ref[chosen[slot]]


def select(attend, rows, slots):
    return pl.pallas_call(
        select_kernel,
        in_specs=[pl.BlockSpec(memory_space=pltpu.SMEM), pl.BlockSpec(memory_space=pltpu.VMEM)],
        out_specs=[pl.BlockSpec(memory_space=pltpu.VMEM), pl.BlockSpec(memory_space=pltpu.SMEM)],
        out_shape=[
            jax.ShapeDtypeStruct((CS, slots, *rows.shape[1:]), rows.dtype),
            jax.ShapeDtypeStruct((2, attend.shape[0]), jnp.int32),
        ],
    )(attend, rows)


def visit_kernel(heads, span, plan, rows_ref, key_ref, value_ref, out_q, out_k, out_v):
    question = pl.program_id(0)
    scale = WIDTH**-0.5

    @pl.when(question == 0)
    def _():
        out_k[...] = jnp.zeros_like(out_k)
        out_v[...] = jnp.zeros_like(out_v)

    @pl.when(plan[0, question] == 0)
    def _():
        out_q[...] = jnp.zeros_like(out_q)

    @pl.when(plan[0, question] != 0)
    def _():
        key = key_ref[...]
        value = value_ref[...]
        key_t = key.astype(jnp.float32).T.astype(jnp.bfloat16)
        columns = lax.broadcasted_iota(jnp.int32, (span, WIDTH), 1)
        grad_k = jnp.zeros((span, WIDTH), jnp.float32)
        grad_v = jnp.zeros((span, WIDTH), jnp.float32)

        def take(start):
            return rows_ref[:, 0, :, :, start : start + WIDTH].reshape(ASK_LEN, WIDTH)

        side = take(2 * heads * WIDTH)
        for head in range(heads):
            query = take(head * WIDTH)
            cotangent = take((heads + head) * WIDTH)
            for_shift = (columns < 3 * heads) & (columns % heads == head)
            for_delta = (columns >= 3 * heads) & (columns < 6 * heads) & (columns % heads == head)
            minus_s = jnp.where(for_shift, -1.0, 0.0).astype(jnp.bfloat16)
            minus_d = jnp.where(for_delta, -1.0, 0.0).astype(jnp.bfloat16)
            energy = lax.dot_general(
                jnp.concatenate([key, minus_s], axis=1),
                jnp.concatenate([query, side], axis=1),
                (((1,), (1,)), ((), ())),
                preferred_element_type=jnp.float32,
            )
            prob = jnp.exp2(energy * (scale * LOG2E))
            change = lax.dot_general(
                jnp.concatenate([value, minus_d], axis=1),
                jnp.concatenate([cotangent, side], axis=1),
                (((1,), (1,)), ((), ())),
                preferred_element_type=jnp.float32,
            )
            low_score = (prob * change).astype(jnp.bfloat16)
            low_prob = prob.astype(jnp.bfloat16)
            grad_k = grad_k + jnp.dot(low_score, query, preferred_element_type=jnp.float32)
            grad_v = grad_v + jnp.dot(low_prob, cotangent, preferred_element_type=jnp.float32)
            term = jnp.dot(key_t, low_score, preferred_element_type=jnp.float32).T * scale
            term = term.astype(jnp.bfloat16)
            place = slice(head * WIDTH, (head + 1) * WIDTH)
            out_q[:, 0, :, :, place] = term.reshape(out_q.shape[0], out_q.shape[2], out_q.shape[3], WIDTH)
        out_k[...] += grad_k * scale
        out_v[...] += grad_v


def visits(plan, rows, keys, values, heads):
    cores, _, chunks, chunk, packed = rows.shape
    questions = plan.shape[1]
    span = keys.shape[0]
    columns = heads * WIDTH
    whole = pl.BlockSpec((span, WIDTH), lambda n, p: (0, 0))
    return pl.pallas_call(
        functools.partial(visit_kernel, heads, span),
        grid_spec=pltpu.PrefetchScalarGridSpec(
            num_scalar_prefetch=1,
            grid=(questions,),
            in_specs=[
                pl.BlockSpec((cores, 1, chunks, chunk, packed), lambda n, p: (0, p[1, n], 0, 0, 0)),
                whole,
                whole,
            ],
            out_specs=[
                pl.BlockSpec((cores, 1, chunks, chunk, columns), lambda n, p: (0, n, 0, 0, 0)),
                whole,
                whole,
            ],
        ),
        out_shape=[
            jax.ShapeDtypeStruct((cores, questions, chunks, chunk, columns), jnp.bfloat16),
            jax.ShapeDtypeStruct((span, WIDTH), jnp.float32),
            jax.ShapeDtypeStruct((span, WIDTH), jnp.float32),
        ],
        compiler_params=pltpu.CompilerParams(vmem_limit_bytes=40 * 2**20),
    )(plan, rows, keys, values)


def hidden_kernel(query_ref, own_ref, other_ref, out_ref):
    core = lax.rem(lax.axis_index("psg"), CS)
    parts, _, wide = out_ref.shape
    blocks = own_ref.shape[0] // parts

    def product(first_ref, second_ref):
        for part in range(parts):
            here = pl.ds(part * blocks, blocks)
            weight = jnp.concatenate([first_ref[here], second_ref[here]], axis=1)
            out_ref[part] = lax.dot_general(
                query_ref[...],
                weight.reshape(wide, weight.shape[2]),
                (((1,), (1,)), ((), ())),
                preferred_element_type=jnp.float32,
            ).astype(out_ref.dtype)

    @pl.when(core == 0)
    def _():
        product(own_ref, other_ref)

    @pl.when(core != 0)
    def _():
        product(other_ref, own_ref)


def hidden_parts(query_low, own, other, parts):
    rows, columns = query_low.shape
    chips, height, _ = own.shape
    wide = CS * chips * height // parts
    steps = 4
    weights = pl.BlockSpec((chips // steps, height, columns), lambda n: (n, 0, 0))
    return pl.pallas_call(
        hidden_kernel,
        grid=(steps,),
        in_specs=[pl.BlockSpec((rows, columns), lambda n: (0, 0)), weights, weights],
        out_specs=pl.BlockSpec((parts // steps, rows, wide), lambda n: (n, 0, 0)),
        out_shape=jax.ShapeDtypeStruct((parts, rows, wide), jnp.bfloat16),
        compiler_params=pltpu.CompilerParams(vmem_limit_bytes=WIDE),
    )(query_low, own, other)


def on_device(queries, grad_out, attn_out, log_sum, keys, values, proj_weight, attend, qlen):
    heads = log_sum.shape[0]
    rows, columns = queries.shape
    packed = pack_rows(queries, grad_out, attn_out, log_sum, qlen, ZS)
    line = spread(packed, "psg", Z_GROUPS)
    gathered = spread(jnp.broadcast_to(line[None], (XS, *line.shape)), "psg", X_GROUPS)
    question_total, top = attend.shape
    gathered, proj_weight = lax.optimization_barrier((gathered, proj_weight))
    own_weight = lax.all_gather(proj_weight, "psg", axis=0, axis_index_groups=CORE_GROUPS)
    gathered = gathered.reshape(question_total, -1, rows, packed.shape[2])
    slots = min(question_total, 2 * question_total * top // (XS * ZS * CS))
    chosen, plan = select(attend, gathered, slots)
    chosen = spread(chosen, "psg", C_GROUPS)

    terms, grad_keys, grad_values = visits(plan, chosen, keys, values, heads)

    terms = spread(terms, "psg", C_GROUPS)
    pair = jnp.sum(terms.astype(jnp.float32), axis=0).astype(jnp.bfloat16)
    pair = spread(pair.reshape(XS, ZS, rows, columns), "psg", X_GROUPS)
    line = jnp.sum(pair.astype(jnp.float32), axis=0).astype(jnp.bfloat16)
    line, own_weight = lax.optimization_barrier((line, own_weight))
    other_weight = lax.ppermute(own_weight, "psg", CORE_SWAP)
    line = spread(line, "psg", Z_GROUPS)
    grad_query = jnp.sum(line.astype(jnp.float32), axis=0)
    query_low = grad_query.astype(jnp.bfloat16)

    parts = lax.axis_size("qry")
    terms = hidden_parts(query_low, own_weight, other_weight, parts)
    terms = spread(terms, "qry", None)
    hidden = jnp.sum(terms.astype(jnp.float32), axis=0)
    hidden = spread(jnp.broadcast_to(hidden[None], (parts, *hidden.shape)), "qry", None)
    grad_hidden = jnp.swapaxes(hidden, 0, 1).reshape(rows, -1)
    return (grad_query, grad_keys, grad_values, grad_hidden)


def solution(mesh):
    in_specs = (
        P("psg", "qry"),
        P("psg", "qry"),
        P("psg", "qry"),
        P("qry", "psg"),
        P("psg", "qry"),
        P("psg", "qry"),
        P("psg", "qry"),
        P(),
        P(),
    )
    out_specs = (P("psg", "qry"), P("psg", "qry"), P("psg", "qry"), P("psg", None))
    return jax.shard_map(
        on_device, mesh=mesh, in_specs=in_specs, out_specs=out_specs, check_vma=False
    )
```

```python
import functools

import jax
import jax.numpy as jnp
from jax import lax
from jax.experimental import pallas as pl
from jax.experimental.pallas import tpu as pltpu
from jax.sharding import PartitionSpec as P

WIDTH = 128
GROUP = 4
ASK_LEN = 256
XS, ZS, CS = 4, 8, 2
LOG2E = 1.4426950408889634
FAR = 1.0e6
WIDE = 63 * 2**20


def index_of(x, z, c):
    return (x * ZS + z) * CS + c


Z_GROUPS = [[index_of(x, z, c) for z in range(ZS)] for x in range(XS) for c in range(CS)]
X_GROUPS = [[index_of(x, z, c) for x in range(XS)] for z in range(ZS) for c in range(CS)]
C_GROUPS = [[index_of(x, z, c) for c in range(CS)] for x in range(XS) for z in range(ZS)]

PLANE_GROUPS = [[index_of(x, z, c) for x in range(XS) for z in range(ZS)] for c in range(CS)]


def spread(blocks, axis, groups):
    return lax.all_to_all(blocks, axis, 0, 0, tiled=True, axis_index_groups=groups)


def pack_kernel(heads, qlen_ref, query_in, grad_in, output_in, lse_in, out_ref, query_ref, grad_ref, output_ref, lse_ref, sems):
    copies = [
        pltpu.make_async_copy(source, target, sems.at[k])
        for k, (source, target) in enumerate(
            ((grad_in, grad_ref), (output_in, output_ref), (lse_in, lse_ref), (query_in, query_ref))
        )
    ]
    for copy in copies:
        copy.start()
    rows, columns = query_ref.shape
    shape = (rows, WIDTH)
    owner = lax.axis_index("psg")
    per_question = ASK_LEN // rows
    question = lax.div(owner, per_question)
    first = (owner - question * per_question) * rows
    column = lax.broadcasted_iota(jnp.int32, shape, 1)
    row = lax.broadcasted_iota(jnp.int32, shape, 0)
    live = first + row < qlen_ref[question]
    square = lax.broadcasted_iota(jnp.int32, (rows, rows), 0) == lax.broadcasted_iota(jnp.int32, (rows, rows), 1)
    value = jnp.zeros(shape, jnp.float32)
    for copy in copies:
        copy.wait()
    for head in range(heads):
        part = slice(head * WIDTH, (head + 1) * WIDTH)
        products = grad_ref[:, part].astype(jnp.float32) * output_ref[:, part].astype(jnp.float32)
        delta = jnp.sum(products, axis=1, keepdims=True)
        spread_lse = jnp.broadcast_to(lse_ref[head : head + 1, :], (rows, rows))
        shift = jnp.sum(jnp.where(square, spread_lse, 0.0), axis=1, keepdims=True) * (WIDTH**0.5)
        shift = jnp.where(live, shift, FAR)
        value = jnp.where(column % heads == head, jnp.where(column < 3 * heads, shift, delta), value)
    high = value.astype(jnp.bfloat16).astype(jnp.float32)
    middle = (value - high).astype(jnp.bfloat16).astype(jnp.float32)
    low = value - high - middle
    piece = (column // heads) % 3
    side = jnp.where(piece == 0, high, jnp.where(piece == 1, middle, low))
    side = jnp.where(column < 6 * heads, side, 0.0).astype(jnp.bfloat16)
    for copy in range(out_ref.shape[0]):
        out_ref[copy, :, :columns] = query_ref[...]
        out_ref[copy, :, columns : 2 * columns] = grad_ref[...]
        out_ref[copy, :, 2 * columns :] = side


def pack_rows(queries, grad_out, attn_out, log_sum, qlen, copies):
    rows, columns = queries.shape
    heads = log_sum.shape[0]
    anywhere = pl.BlockSpec(memory_space=pl.ANY)
    return pl.pallas_call(
        functools.partial(pack_kernel, heads),
        in_specs=[pl.BlockSpec(memory_space=pltpu.SMEM)] + [anywhere] * 4,
        out_specs=pl.BlockSpec(memory_space=pltpu.VMEM),
        out_shape=jax.ShapeDtypeStruct((copies, rows, 2 * columns + WIDTH), jnp.bfloat16),
        scratch_shapes=[
            pltpu.VMEM((rows, columns), jnp.bfloat16),
            pltpu.VMEM((rows, columns), jnp.bfloat16),
            pltpu.VMEM((rows, columns), jnp.bfloat16),
            pltpu.VMEM((heads, rows), jnp.float32),
            pltpu.SemaphoreType.DMA((4,)),
        ],
        compiler_params=pltpu.CompilerParams(vmem_limit_bytes=WIDE),
    )(qlen, queries, grad_out, attn_out, log_sum)


def select_kernel(attend_ref, rows_ref, out_ref, plan_ref):
    questions, top = attend_ref.shape
    slots = out_ref.shape[1]
    owner = lax.axis_index("psg")
    core = lax.rem(owner, CS)
    for target in range(CS):
        block = owner - core + target
        count = jnp.int32(0)
        chosen = [jnp.int32(0)] * slots
        for question in range(questions):
            hit = jnp.int32(0)
            for place in range(top):
                hit = hit | (attend_ref[question, place] == block).astype(jnp.int32)
            chosen = [jnp.where((hit == 1) & (count == k), question, chosen[k]) for k in range(slots)]
            count = count + hit

            @pl.when(core == target)
            def _():
                plan_ref[0, question] = hit
                plan_ref[1, question] = jnp.clip(count - 1, 0, slots - 1)

        for slot in range(slots):
            out_ref[target, slot] = rows_ref[chosen[slot]]


def select(attend, rows, slots):
    return pl.pallas_call(
        select_kernel,
        in_specs=[pl.BlockSpec(memory_space=pltpu.SMEM), pl.BlockSpec(memory_space=pltpu.VMEM)],
        out_specs=[pl.BlockSpec(memory_space=pltpu.VMEM), pl.BlockSpec(memory_space=pltpu.SMEM)],
        out_shape=[
            jax.ShapeDtypeStruct((CS, slots, *rows.shape[1:]), rows.dtype),
            jax.ShapeDtypeStruct((2, attend.shape[0]), jnp.int32),
        ],
        compiler_params=pltpu.CompilerParams(vmem_limit_bytes=16 * 2**20),
    )(attend, rows)


def visit_kernel(heads, span, plan, rows_ref, key_ref, value_ref, out_q, out_k, out_v):
    question = pl.program_id(0)
    scale = WIDTH**-0.5

    @pl.when(question == 0)
    def _():
        out_k[...] = jnp.zeros_like(out_k)
        out_v[...] = jnp.zeros_like(out_v)

    @pl.when(plan[0, question] == 0)
    def _():
        out_q[...] = jnp.zeros_like(out_q)

    @pl.when(plan[0, question] != 0)
    def _():
        key = key_ref[...]
        value = value_ref[...]
        key_t = key.astype(jnp.float32).T.astype(jnp.bfloat16)
        columns = lax.broadcasted_iota(jnp.int32, (span, WIDTH), 1)
        grad_k = jnp.zeros((span, WIDTH), jnp.float32)
        grad_v = jnp.zeros((span, WIDTH), jnp.float32)

        def take(start):
            return rows_ref[:, 0, :, :, start : start + WIDTH].reshape(ASK_LEN, WIDTH)

        side = take(2 * heads * WIDTH)
        for head in range(heads):
            query = take(head * WIDTH)
            cotangent = take((heads + head) * WIDTH)
            for_shift = (columns < 3 * heads) & (columns % heads == head)
            for_delta = (columns >= 3 * heads) & (columns < 6 * heads) & (columns % heads == head)
            minus_s = jnp.where(for_shift, -1.0, 0.0).astype(jnp.bfloat16)
            minus_d = jnp.where(for_delta, -1.0, 0.0).astype(jnp.bfloat16)
            energy = lax.dot_general(
                jnp.concatenate([key, minus_s], axis=1),
                jnp.concatenate([query, side], axis=1),
                (((1,), (1,)), ((), ())),
                preferred_element_type=jnp.float32,
            )
            prob = jnp.exp2(energy * (scale * LOG2E))
            change = lax.dot_general(
                jnp.concatenate([value, minus_d], axis=1),
                jnp.concatenate([cotangent, side], axis=1),
                (((1,), (1,)), ((), ())),
                preferred_element_type=jnp.float32,
            )
            low_score = (prob * change).astype(jnp.bfloat16)
            low_prob = prob.astype(jnp.bfloat16)
            grad_k = grad_k + jnp.dot(low_score, query, preferred_element_type=jnp.float32)
            grad_v = grad_v + jnp.dot(low_prob, cotangent, preferred_element_type=jnp.float32)
            term = jnp.dot(key_t, low_score, preferred_element_type=jnp.float32).T * scale
            term = term.astype(jnp.bfloat16)
            place = slice(head * WIDTH, (head + 1) * WIDTH)
            out_q[:, 0, :, :, place] = term.reshape(out_q.shape[0], out_q.shape[2], out_q.shape[3], WIDTH)
        out_k[...] += grad_k * scale
        out_v[...] += grad_v


def visits(plan, rows, keys, values, heads):
    cores, _, chunks, chunk, packed = rows.shape
    questions = plan.shape[1]
    span = keys.shape[0]
    columns = heads * WIDTH
    whole = pl.BlockSpec((span, WIDTH), lambda n, p: (0, 0))
    return pl.pallas_call(
        functools.partial(visit_kernel, heads, span),
        grid_spec=pltpu.PrefetchScalarGridSpec(
            num_scalar_prefetch=1,
            grid=(questions,),
            in_specs=[
                pl.BlockSpec((cores, 1, chunks, chunk, packed), lambda n, p: (0, p[1, n], 0, 0, 0)),
                whole,
                whole,
            ],
            out_specs=[
                pl.BlockSpec((cores, 1, chunks, chunk, columns), lambda n, p: (0, n, 0, 0, 0)),
                whole,
                whole,
            ],
        ),
        out_shape=[
            jax.ShapeDtypeStruct((cores, questions, chunks, chunk, columns), jnp.bfloat16),
            jax.ShapeDtypeStruct((span, WIDTH), jnp.float32),
            jax.ShapeDtypeStruct((span, WIDTH), jnp.float32),
        ],
        compiler_params=pltpu.CompilerParams(vmem_limit_bytes=32 * 2**20),
    )(plan, rows, keys, values)


def hidden_kernel(query_ref, weight_ref, out_ref):
    parts, _, wide = out_ref.shape
    for part in range(parts):
        out_ref[part] = lax.dot_general(
            query_ref[...],
            weight_ref[pl.ds(part * wide, wide)],
            (((1,), (1,)), ((), ())),
            preferred_element_type=jnp.float32,
        ).astype(out_ref.dtype)


def hidden_parts(query_low, weight, parts):
    rows, columns = query_low.shape
    total = weight.shape[0]
    wide = total // parts
    steps = 4
    return pl.pallas_call(
        hidden_kernel,
        grid=(steps,),
        in_specs=[
            pl.BlockSpec((rows, columns), lambda n: (0, 0)),
            pl.BlockSpec((total // steps, columns), lambda n: (n, 0)),
        ],
        out_specs=pl.BlockSpec((parts // steps, rows, wide), lambda n: (n, 0, 0)),
        out_shape=jax.ShapeDtypeStruct((parts, rows, wide), jnp.bfloat16),
        compiler_params=pltpu.CompilerParams(vmem_limit_bytes=60 * 2**20),
    )(query_low, weight)


def on_device(queries, grad_out, attn_out, log_sum, keys, values, proj_weight, attend, qlen):
    heads = log_sum.shape[0]
    rows, columns = queries.shape
    weight = lax.all_gather(proj_weight, "psg", axis=0, tiled=True)

    packed = pack_rows(queries, grad_out, attn_out, log_sum, qlen, ZS)
    line = spread(packed, "psg", Z_GROUPS)
    gathered = spread(jnp.broadcast_to(line[None], (XS, *line.shape)), "psg", X_GROUPS)
    question_total, top = attend.shape
    gathered = gathered.reshape(question_total, -1, rows, packed.shape[2])
    slots = min(question_total, 2 * question_total * top // (XS * ZS * CS))
    chosen, plan = select(attend, gathered, slots)
    chosen = spread(chosen, "psg", C_GROUPS)

    terms, grad_keys, grad_values = visits(plan, chosen, keys, values, heads)

    terms = spread(terms, "psg", C_GROUPS)
    pair = jnp.sum(terms.astype(jnp.float32), axis=0).astype(jnp.bfloat16)
    plane = spread(pair.reshape(XS * ZS, rows, columns), "psg", PLANE_GROUPS)
    grad_query = jnp.sum(plane.astype(jnp.float32), axis=0)
    query_low = grad_query.astype(jnp.bfloat16)

    parts = lax.axis_size("qry")
    terms = hidden_parts(query_low, weight, parts)
    terms = spread(terms, "qry", None)
    hidden = jnp.sum(terms.astype(jnp.float32), axis=0).astype(jnp.bfloat16)
    hidden = spread(jnp.broadcast_to(hidden[None], (parts, *hidden.shape)), "qry", None)
    grad_hidden = jnp.swapaxes(hidden.astype(jnp.float32), 0, 1).reshape(rows, -1)
    return (grad_query, grad_keys, grad_values, grad_hidden)


def solution(mesh):
    in_specs = (
        P("psg", "qry"),
        P("psg", "qry"),
        P("psg", "qry"),
        P("qry", "psg"),
        P("psg", "qry"),
        P("psg", "qry"),
        P("psg", "qry"),
        P(),
        P(),
    )
    out_specs = (P("psg", "qry"), P("psg", "qry"), P("psg", "qry"), P("psg", None))
    return jax.shard_map(
        on_device, mesh=mesh, in_specs=in_specs, out_specs=out_specs, check_vma=False
    )
```

```python
import functools

import jax
import jax.numpy as jnp
from jax import lax
from jax.experimental import pallas as pl
from jax.experimental.pallas import tpu as pltpu
from jax.sharding import PartitionSpec as P

WIDTH = 128
GROUP = 4
ASK_LEN = 256
XS, ZS, CS = 4, 8, 2
LOG2E = 1.4426950408889634
FAR = 1.0e6
WIDE = 63 * 2**20


def index_of(x, z, c):
    return (x * ZS + z) * CS + c


Z_GROUPS = [[index_of(x, z, c) for z in range(ZS)] for x in range(XS) for c in range(CS)]
X_GROUPS = [[index_of(x, z, c) for x in range(XS)] for z in range(ZS) for c in range(CS)]
C_GROUPS = [[index_of(x, z, c) for c in range(CS)] for x in range(XS) for z in range(ZS)]

PLANE_GROUPS = [[index_of(x, z, c) for x in range(XS) for z in range(ZS)] for c in range(CS)]

CORE_SWAP = [(i, i ^ 1) for i in range(XS * ZS * CS)]
X_STEPS = [
    [(index_of(x, z, c), index_of((x + k) % XS, z, c)) for x in range(XS) for z in range(ZS) for c in range(CS)]
    for k in range(1, XS)
]


def z_step(k):
    return [
        (index_of(x, z, c), index_of(x, (z + k) % ZS, c)) for x in range(XS) for z in range(ZS) for c in range(CS)
    ]


def spread(blocks, axis, groups):
    return lax.all_to_all(blocks, axis, 0, 0, tiled=True, axis_index_groups=groups)


def pack_kernel(heads, qlen_ref, query_in, grad_in, output_in, lse_in, out_ref, query_ref, grad_ref, output_ref, lse_ref, sems):
    copies = [
        pltpu.make_async_copy(source, target, sems.at[k])
        for k, (source, target) in enumerate(
            ((grad_in, grad_ref), (output_in, output_ref), (lse_in, lse_ref), (query_in, query_ref))
        )
    ]
    for copy in copies:
        copy.start()
    rows, columns = query_ref.shape
    shape = (rows, WIDTH)
    owner = lax.axis_index("psg")
    per_question = ASK_LEN // rows
    question = lax.div(owner, per_question)
    first = (owner - question * per_question) * rows
    column = lax.broadcasted_iota(jnp.int32, shape, 1)
    row = lax.broadcasted_iota(jnp.int32, shape, 0)
    live = first + row < qlen_ref[question]
    square = lax.broadcasted_iota(jnp.int32, (rows, rows), 0) == lax.broadcasted_iota(jnp.int32, (rows, rows), 1)
    value = jnp.zeros(shape, jnp.float32)
    for copy in copies:
        copy.wait()
    for head in range(heads):
        part = slice(head * WIDTH, (head + 1) * WIDTH)
        products = grad_ref[:, part].astype(jnp.float32) * output_ref[:, part].astype(jnp.float32)
        delta = jnp.sum(products, axis=1, keepdims=True)
        spread_lse = jnp.broadcast_to(lse_ref[head : head + 1, :], (rows, rows))
        shift = jnp.sum(jnp.where(square, spread_lse, 0.0), axis=1, keepdims=True) * (WIDTH**0.5)
        shift = jnp.where(live, shift, FAR)
        value = jnp.where(column % heads == head, jnp.where(column < 3 * heads, shift, delta), value)
    high = value.astype(jnp.bfloat16).astype(jnp.float32)
    middle = (value - high).astype(jnp.bfloat16).astype(jnp.float32)
    low = value - high - middle
    piece = (column // heads) % 3
    side = jnp.where(piece == 0, high, jnp.where(piece == 1, middle, low))
    side = jnp.where(column < 6 * heads, side, 0.0).astype(jnp.bfloat16)
    for copy in range(out_ref.shape[0]):
        out_ref[copy, :, :columns] = query_ref[...]
        out_ref[copy, :, columns : 2 * columns] = grad_ref[...]
        out_ref[copy, :, 2 * columns :] = side


def pack_rows(queries, grad_out, attn_out, log_sum, qlen, copies):
    rows, columns = queries.shape
    heads = log_sum.shape[0]
    anywhere = pl.BlockSpec(memory_space=pl.ANY)
    return pl.pallas_call(
        functools.partial(pack_kernel, heads),
        in_specs=[pl.BlockSpec(memory_space=pltpu.SMEM)] + [anywhere] * 4,
        out_specs=pl.BlockSpec(memory_space=pltpu.VMEM),
        out_shape=jax.ShapeDtypeStruct((copies, rows, 2 * columns + WIDTH), jnp.bfloat16),
        scratch_shapes=[
            pltpu.VMEM((rows, columns), jnp.bfloat16),
            pltpu.VMEM((rows, columns), jnp.bfloat16),
            pltpu.VMEM((rows, columns), jnp.bfloat16),
            pltpu.VMEM((heads, rows), jnp.float32),
            pltpu.SemaphoreType.DMA((4,)),
        ],
        compiler_params=pltpu.CompilerParams(vmem_limit_bytes=WIDE),
    )(qlen, queries, grad_out, attn_out, log_sum)


def select_kernel(attend_ref, rows_ref, out_ref, plan_ref):
    questions, top = attend_ref.shape
    slots = out_ref.shape[1]
    owner = lax.axis_index("psg")
    core = lax.rem(owner, CS)
    for target in range(CS):
        block = owner - core + target
        count = jnp.int32(0)
        chosen = [jnp.int32(0)] * slots
        for question in range(questions):
            hit = jnp.int32(0)
            for place in range(top):
                hit = hit | (attend_ref[question, place] == block).astype(jnp.int32)
            chosen = [jnp.where((hit == 1) & (count == k), question, chosen[k]) for k in range(slots)]
            count = count + hit

            @pl.when(core == target)
            def _():
                plan_ref[0, question] = hit
                plan_ref[1, question] = jnp.clip(count - 1, 0, slots - 1)

        for slot in range(slots):
            out_ref[target, slot] = rows_ref[chosen[slot]]


def select(attend, rows, slots):
    return pl.pallas_call(
        select_kernel,
        in_specs=[pl.BlockSpec(memory_space=pltpu.SMEM), pl.BlockSpec(memory_space=pltpu.VMEM)],
        out_specs=[pl.BlockSpec(memory_space=pltpu.VMEM), pl.BlockSpec(memory_space=pltpu.SMEM)],
        out_shape=[
            jax.ShapeDtypeStruct((CS, slots, *rows.shape[1:]), rows.dtype),
            jax.ShapeDtypeStruct((2, attend.shape[0]), jnp.int32),
        ],
        compiler_params=pltpu.CompilerParams(vmem_limit_bytes=16 * 2**20),
    )(attend, rows)


def visit_kernel(heads, plan, rows_ref, key_ref, value_ref, out_q, out_k, out_v):
    scale = WIDTH**-0.5
    span = key_ref.shape[0]
    cores, questions, chunks, chunk, _ = out_q.shape
    out_k[...] = jnp.zeros_like(out_k)
    out_v[...] = jnp.zeros_like(out_v)
    key_t = key_ref[...].astype(jnp.float32).T.astype(jnp.bfloat16)
    columns = lax.broadcasted_iota(jnp.int32, (span, WIDTH), 1)

    @pl.loop(0, questions)
    def _(question):
        slot = plan[1, question]

        def take(start):
            return rows_ref[:, slot, :, :, start : start + WIDTH].reshape(ASK_LEN, WIDTH)

        @pl.when(plan[0, question] == 0)
        def _():
            out_q[:, question] = jnp.zeros((cores, chunks, chunk, heads * WIDTH), out_q.dtype)

        @pl.when(plan[0, question] != 0)
        def _():
            key = key_ref[...]
            value = value_ref[...]
            grad_k = jnp.zeros((span, WIDTH), jnp.float32)
            grad_v = jnp.zeros((span, WIDTH), jnp.float32)
            side = take(2 * heads * WIDTH)
            for head in range(heads):
                query = take(head * WIDTH)
                cotangent = take((heads + head) * WIDTH)
                for_shift = (columns < 3 * heads) & (columns % heads == head)
                for_delta = (columns >= 3 * heads) & (columns < 6 * heads) & (columns % heads == head)
                minus_s = jnp.where(for_shift, -1.0, 0.0).astype(jnp.bfloat16)
                minus_d = jnp.where(for_delta, -1.0, 0.0).astype(jnp.bfloat16)
                energy = lax.dot_general(
                    jnp.concatenate([key, minus_s], axis=1),
                    jnp.concatenate([query, side], axis=1),
                    (((1,), (1,)), ((), ())),
                    preferred_element_type=jnp.float32,
                )
                prob = jnp.exp2(energy * (scale * LOG2E))
                change = lax.dot_general(
                    jnp.concatenate([value, minus_d], axis=1),
                    jnp.concatenate([cotangent, side], axis=1),
                    (((1,), (1,)), ((), ())),
                    preferred_element_type=jnp.float32,
                )
                low_score = (prob * change).astype(jnp.bfloat16)
                low_prob = prob.astype(jnp.bfloat16)
                grad_k = grad_k + jnp.dot(low_score, query, preferred_element_type=jnp.float32)
                grad_v = grad_v + jnp.dot(low_prob, cotangent, preferred_element_type=jnp.float32)
                term = jnp.dot(key_t, low_score, preferred_element_type=jnp.float32).T * scale
                term = term.astype(jnp.bfloat16).reshape(cores, chunks, chunk, WIDTH)
                out_q[:, question, :, :, head * WIDTH : (head + 1) * WIDTH] = term
            out_k[...] += grad_k * scale
            out_v[...] += grad_v


def visits(plan, rows, keys, values, heads):
    cores, _, chunks, chunk, _ = rows.shape
    vmem = pl.BlockSpec(memory_space=pltpu.VMEM)
    return pl.pallas_call(
        functools.partial(visit_kernel, heads),
        in_specs=[pl.BlockSpec(memory_space=pltpu.SMEM), vmem, vmem, vmem],
        out_specs=[vmem, vmem, vmem],
        out_shape=[
            jax.ShapeDtypeStruct((cores, plan.shape[1], chunks, chunk, heads * WIDTH), jnp.bfloat16),
            jax.ShapeDtypeStruct(keys.shape, jnp.float32),
            jax.ShapeDtypeStruct(values.shape, jnp.float32),
        ],
        compiler_params=pltpu.CompilerParams(vmem_limit_bytes=32 * 2**20),
    )(plan, rows, keys, values)


def hidden_kernel(query_ref, own_ref, other_ref, out_ref):
    place = lax.axis_index("psg")
    core = lax.rem(place, CS)
    z = lax.rem(lax.div(place, CS), ZS)
    x = lax.div(place, CS * ZS)
    parts, _, wide = out_ref.shape
    depth = query_ref.shape[1]
    per_part = XS * ZS // parts

    def product(first_ref, second_ref):
        query = query_ref[...].astype(jnp.bfloat16)
        for part in range(parts):
            blocks = []
            for chip in range(part * per_part, (part + 1) * per_part):
                far_x = lax.rem(x - chip // ZS + XS, XS)
                off_z = lax.rem(chip % ZS - z + ZS, ZS)
                base = jnp.where(off_z < 2, XS - XS * off_z, (ZS + 1 - off_z) * XS)
                blocks += [first_ref[base + far_x], second_ref[base + far_x]]
            out_ref[part] = lax.dot_general(
                query,
                jnp.concatenate(blocks, axis=0).reshape(wide, depth),
                (((1,), (1,)), ((), ())),
                preferred_element_type=jnp.float32,
            ).astype(out_ref.dtype)

    @pl.when(core == 0)
    def _():
        product(own_ref, other_ref)

    @pl.when(core != 0)
    def _():
        product(other_ref, own_ref)


def hidden_parts(grad_query, own, other, parts):
    rows = grad_query.shape[0]
    wide = CS * own.shape[0] * own.shape[1] // parts
    vmem = pl.BlockSpec(memory_space=pltpu.VMEM)
    return pl.pallas_call(
        hidden_kernel,
        in_specs=[vmem, vmem, vmem],
        out_specs=vmem,
        out_shape=jax.ShapeDtypeStruct((parts, rows, wide), jnp.bfloat16),
        compiler_params=pltpu.CompilerParams(vmem_limit_bytes=16 * 2**20),
    )(grad_query, own, other)


def on_device(queries, grad_out, attn_out, log_sum, keys, values, proj_weight, attend, qlen):
    heads = log_sum.shape[0]
    rows, columns = queries.shape
    packed = pack_rows(queries, grad_out, attn_out, log_sum, qlen, ZS)
    packed, proj_weight = lax.optimization_barrier((packed, proj_weight))
    line = spread(packed, "psg", Z_GROUPS)
    near = jnp.stack([proj_weight] + [lax.ppermute(proj_weight, "psg", steps) for steps in X_STEPS])
    line, near = lax.optimization_barrier((line, near))
    gathered = spread(jnp.broadcast_to(line[None], (XS, *line.shape)), "psg", X_GROUPS)
    trio = jnp.concatenate(
        [lax.ppermute(near, "psg", z_step(-1)), near, lax.ppermute(near, "psg", z_step(1))], axis=0
    )
    share = 5 * XS // 2
    below = lax.ppermute(trio[:share], "psg", z_step(3))
    above = lax.ppermute(trio[-share:], "psg", z_step(-3))
    question_total, top = attend.shape
    gathered = gathered.reshape(question_total, -1, rows, packed.shape[2])
    slots = min(question_total, 2 * question_total * top // (XS * ZS * CS))
    chosen, plan = select(attend, gathered, slots)
    chosen = spread(chosen, "psg", C_GROUPS)

    terms, grad_keys, grad_values = visits(plan, chosen, keys, values, heads)

    terms = spread(terms, "psg", C_GROUPS)
    pair = jnp.sum(terms.astype(jnp.float32), axis=0).astype(jnp.bfloat16)
    _, trio, below, above = lax.optimization_barrier((pair, trio, below, above))
    plane = spread(pair.reshape(XS * ZS, rows, columns), "psg", PLANE_GROUPS)
    own_weight = jnp.concatenate([trio, below, above], axis=0)
    other_weight = lax.ppermute(own_weight, "psg", CORE_SWAP)
    grad_query = jnp.sum(plane.astype(jnp.float32), axis=0)

    parts = lax.axis_size("qry")
    terms = hidden_parts(grad_query, own_weight, other_weight, parts)
    terms = spread(terms, "qry", None)
    hidden = jnp.sum(terms.astype(jnp.float32), axis=0).astype(jnp.bfloat16)
    hidden = spread(jnp.broadcast_to(hidden[None], (parts, *hidden.shape)), "qry", None)
    grad_hidden = jnp.swapaxes(hidden.astype(jnp.float32), 0, 1).reshape(rows, -1)
    return (grad_query, grad_keys, grad_values, grad_hidden)


def solution(mesh):
    in_specs = (
        P("psg", "qry"),
        P("psg", "qry"),
        P("psg", "qry"),
        P("qry", "psg"),
        P("psg", "qry"),
        P("psg", "qry"),
        P("psg", "qry"),
        P(),
        P(),
    )
    out_specs = (P("psg", "qry"), P("psg", "qry"), P("psg", "qry"), P("psg", None))
    return jax.shard_map(
        on_device, mesh=mesh, in_specs=in_specs, out_specs=out_specs, check_vma=False
    )
```

```python
import functools

import jax
import jax.numpy as jnp
from jax import lax
from jax.experimental import pallas as pl
from jax.experimental.pallas import tpu as pltpu
from jax.sharding import PartitionSpec as P

WIDTH = 128
GROUP = 4
ASK_LEN = 256
XS, ZS, CS = 4, 8, 2
LOG2E = 1.4426950408889634
FAR = 1.0e6
WIDE = 63 * 2**20


def index_of(x, z, c):
    return (x * ZS + z) * CS + c


Z_GROUPS = [[index_of(x, z, c) for z in range(ZS)] for x in range(XS) for c in range(CS)]
X_GROUPS = [[index_of(x, z, c) for x in range(XS)] for z in range(ZS) for c in range(CS)]
C_GROUPS = [[index_of(x, z, c) for c in range(CS)] for x in range(XS) for z in range(ZS)]

PLANE_GROUPS = [[index_of(x, z, c) for x in range(XS) for z in range(ZS)] for c in range(CS)]

CORE_SWAP = [(i, i ^ 1) for i in range(XS * ZS * CS)]
X_STEPS = [
    [(index_of(x, z, c), index_of((x + k) % XS, z, c)) for x in range(XS) for z in range(ZS) for c in range(CS)]
    for k in range(1, XS)
]


def z_step(k):
    return [
        (index_of(x, z, c), index_of(x, (z + k) % ZS, c)) for x in range(XS) for z in range(ZS) for c in range(CS)
    ]


def spread(blocks, axis, groups):
    return lax.all_to_all(blocks, axis, 0, 0, tiled=True, axis_index_groups=groups)


def pack_kernel(heads, qlen_ref, query_in, grad_in, output_in, lse_in, out_ref, query_ref, grad_ref, output_ref, lse_ref, sems):
    copies = [
        pltpu.make_async_copy(source, target, sems.at[k])
        for k, (source, target) in enumerate(
            ((grad_in, grad_ref), (output_in, output_ref), (lse_in, lse_ref), (query_in, query_ref))
        )
    ]
    for copy in copies:
        copy.start()
    rows, columns = query_ref.shape
    shape = (rows, WIDTH)
    owner = lax.axis_index("psg")
    per_question = ASK_LEN // rows
    question = lax.div(owner, per_question)
    first = (owner - question * per_question) * rows
    column = lax.broadcasted_iota(jnp.int32, shape, 1)
    row = lax.broadcasted_iota(jnp.int32, shape, 0)
    live = first + row < qlen_ref[question]
    square = lax.broadcasted_iota(jnp.int32, (rows, rows), 0) == lax.broadcasted_iota(jnp.int32, (rows, rows), 1)
    value = jnp.zeros(shape, jnp.float32)
    for copy in copies:
        copy.wait()
    for head in range(heads):
        part = slice(head * WIDTH, (head + 1) * WIDTH)
        products = grad_ref[:, part].astype(jnp.float32) * output_ref[:, part].astype(jnp.float32)
        delta = jnp.sum(products, axis=1, keepdims=True)
        spread_lse = jnp.broadcast_to(lse_ref[head : head + 1, :], (rows, rows))
        shift = jnp.sum(jnp.where(square, spread_lse, 0.0), axis=1, keepdims=True) * (WIDTH**0.5)
        shift = jnp.where(live, shift, FAR)
        value = jnp.where(column % heads == head, jnp.where(column < 3 * heads, shift, delta), value)
    high = value.astype(jnp.bfloat16).astype(jnp.float32)
    middle = (value - high).astype(jnp.bfloat16).astype(jnp.float32)
    low = value - high - middle
    piece = (column // heads) % 3
    side = jnp.where(piece == 0, high, jnp.where(piece == 1, middle, low))
    side = jnp.where(column < 6 * heads, side, 0.0).astype(jnp.bfloat16)
    for copy in range(out_ref.shape[0]):
        out_ref[copy, :, :columns] = query_ref[...]
        out_ref[copy, :, columns : 2 * columns] = grad_ref[...]
        out_ref[copy, :, 2 * columns :] = side


def pack_rows(queries, grad_out, attn_out, log_sum, qlen, copies):
    rows, columns = queries.shape
    heads = log_sum.shape[0]
    anywhere = pl.BlockSpec(memory_space=pl.ANY)
    return pl.pallas_call(
        functools.partial(pack_kernel, heads),
        in_specs=[pl.BlockSpec(memory_space=pltpu.SMEM)] + [anywhere] * 4,
        out_specs=pl.BlockSpec(memory_space=pltpu.VMEM),
        out_shape=jax.ShapeDtypeStruct((copies, rows, 2 * columns + WIDTH), jnp.bfloat16),
        scratch_shapes=[
            pltpu.VMEM((rows, columns), jnp.bfloat16),
            pltpu.VMEM((rows, columns), jnp.bfloat16),
            pltpu.VMEM((rows, columns), jnp.bfloat16),
            pltpu.VMEM((heads, rows), jnp.float32),
            pltpu.SemaphoreType.DMA((4,)),
        ],
        compiler_params=pltpu.CompilerParams(vmem_limit_bytes=WIDE),
    )(qlen, queries, grad_out, attn_out, log_sum)


def select_kernel(attend_ref, rows_ref, out_ref, plan_ref):
    questions, top = attend_ref.shape
    slots = out_ref.shape[1]
    owner = lax.axis_index("psg")
    core = lax.rem(owner, CS)
    for target in range(CS):
        block = owner - core + target
        count = jnp.int32(0)
        chosen = [jnp.int32(0)] * slots
        for question in range(questions):
            hit = jnp.int32(0)
            for place in range(top):
                hit = hit | (attend_ref[question, place] == block).astype(jnp.int32)
            chosen = [jnp.where((hit == 1) & (count == k), question, chosen[k]) for k in range(slots)]
            count = count + hit

            @pl.when(core == target)
            def _():
                plan_ref[0, question] = hit
                plan_ref[1, question] = jnp.clip(count - 1, 0, slots - 1)

        for slot in range(slots):
            out_ref[target, slot] = rows_ref[chosen[slot]]


def select(attend, rows, slots):
    return pl.pallas_call(
        select_kernel,
        in_specs=[pl.BlockSpec(memory_space=pltpu.SMEM), pl.BlockSpec(memory_space=pltpu.VMEM)],
        out_specs=[pl.BlockSpec(memory_space=pltpu.VMEM), pl.BlockSpec(memory_space=pltpu.SMEM)],
        out_shape=[
            jax.ShapeDtypeStruct((CS, slots, *rows.shape[1:]), rows.dtype),
            jax.ShapeDtypeStruct((2, attend.shape[0]), jnp.int32),
        ],
        compiler_params=pltpu.CompilerParams(vmem_limit_bytes=16 * 2**20),
    )(attend, rows)


def visit_kernel(heads, plan, rows_ref, key_ref, value_ref, out_q, out_k, out_v):
    scale = WIDTH**-0.5
    span = key_ref.shape[0]
    cores, questions, chunks, chunk, _ = out_q.shape
    out_k[...] = jnp.zeros_like(out_k)
    out_v[...] = jnp.zeros_like(out_v)
    key_t = key_ref[...].astype(jnp.float32).T.astype(jnp.bfloat16)
    columns = lax.broadcasted_iota(jnp.int32, (span, WIDTH), 1)

    @pl.loop(0, questions)
    def _(question):
        slot = plan[1, question]

        def take(start):
            return rows_ref[:, slot, :, :, start : start + WIDTH].reshape(ASK_LEN, WIDTH)

        @pl.when(plan[0, question] == 0)
        def _():
            out_q[:, question] = jnp.zeros((cores, chunks, chunk, heads * WIDTH), out_q.dtype)

        @pl.when(plan[0, question] != 0)
        def _():
            key = key_ref[...]
            value = value_ref[...]
            grad_k = jnp.zeros((span, WIDTH), jnp.float32)
            grad_v = jnp.zeros((span, WIDTH), jnp.float32)
            side = take(2 * heads * WIDTH)
            for head in range(heads):
                query = take(head * WIDTH)
                cotangent = take((heads + head) * WIDTH)
                for_shift = (columns < 3 * heads) & (columns % heads == head)
                for_delta = (columns >= 3 * heads) & (columns < 6 * heads) & (columns % heads == head)
                minus_s = jnp.where(for_shift, -1.0, 0.0).astype(jnp.bfloat16)
                minus_d = jnp.where(for_delta, -1.0, 0.0).astype(jnp.bfloat16)
                energy = lax.dot_general(
                    jnp.concatenate([key, minus_s], axis=1),
                    jnp.concatenate([query, side], axis=1),
                    (((1,), (1,)), ((), ())),
                    preferred_element_type=jnp.float32,
                )
                prob = jnp.exp2(energy * (scale * LOG2E))
                change = lax.dot_general(
                    jnp.concatenate([value, minus_d], axis=1),
                    jnp.concatenate([cotangent, side], axis=1),
                    (((1,), (1,)), ((), ())),
                    preferred_element_type=jnp.float32,
                )
                low_score = (prob * change).astype(jnp.bfloat16)
                low_prob = prob.astype(jnp.bfloat16)
                grad_k = grad_k + jnp.dot(low_score, query, preferred_element_type=jnp.float32)
                grad_v = grad_v + jnp.dot(low_prob, cotangent, preferred_element_type=jnp.float32)
                term = jnp.dot(key_t, low_score, preferred_element_type=jnp.float32).T * scale
                term = term.astype(jnp.bfloat16).reshape(cores, chunks, chunk, WIDTH)
                out_q[:, question, :, :, head * WIDTH : (head + 1) * WIDTH] = term
            out_k[...] += grad_k * scale
            out_v[...] += grad_v


def visits(plan, rows, keys, values, heads):
    cores, _, chunks, chunk, _ = rows.shape
    vmem = pl.BlockSpec(memory_space=pltpu.VMEM)
    return pl.pallas_call(
        functools.partial(visit_kernel, heads),
        in_specs=[pl.BlockSpec(memory_space=pltpu.SMEM), vmem, vmem, vmem],
        out_specs=[vmem, vmem, vmem],
        out_shape=[
            jax.ShapeDtypeStruct((cores, plan.shape[1], chunks, chunk, heads * WIDTH), jnp.bfloat16),
            jax.ShapeDtypeStruct(keys.shape, jnp.float32),
            jax.ShapeDtypeStruct(values.shape, jnp.float32),
        ],
        compiler_params=pltpu.CompilerParams(vmem_limit_bytes=32 * 2**20),
    )(plan, rows, keys, values)


def hidden_kernel(query_ref, own_ref, other_ref, out_ref):
    place = lax.axis_index("psg")
    core = lax.rem(place, CS)
    z = lax.rem(lax.div(place, CS), ZS)
    x = lax.div(place, CS * ZS)
    parts, _, wide = out_ref.shape
    depth = query_ref.shape[1]
    per_part = XS * ZS // parts

    def product(first_ref, second_ref):
        query = query_ref[...].astype(jnp.bfloat16)
        for part in range(parts):
            blocks = []
            for chip in range(part * per_part, (part + 1) * per_part):
                far_x = lax.rem(x - chip // ZS + XS, XS)
                off_z = lax.rem(chip % ZS - z + ZS, ZS)
                base = (lax.div(off_z, 2) + lax.rem(off_z, 2) * (ZS // 2)) * XS
                blocks += [first_ref[base + far_x], second_ref[base + far_x]]
            out_ref[part] = lax.dot_general(
                query,
                jnp.concatenate(blocks, axis=0).reshape(wide, depth),
                (((1,), (1,)), ((), ())),
                preferred_element_type=jnp.float32,
            ).astype(out_ref.dtype)

    @pl.when(core == 0)
    def _():
        product(own_ref, other_ref)

    @pl.when(core != 0)
    def _():
        product(other_ref, own_ref)


def hidden_parts(grad_query, own, other, parts):
    rows = grad_query.shape[0]
    wide = CS * own.shape[0] * own.shape[1] // parts
    vmem = pl.BlockSpec(memory_space=pltpu.VMEM)
    return pl.pallas_call(
        hidden_kernel,
        in_specs=[vmem, vmem, vmem],
        out_specs=vmem,
        out_shape=jax.ShapeDtypeStruct((parts, rows, wide), jnp.bfloat16),
        compiler_params=pltpu.CompilerParams(vmem_limit_bytes=16 * 2**20),
    )(grad_query, own, other)


def on_device(queries, grad_out, attn_out, log_sum, keys, values, proj_weight, attend, qlen):
    heads = log_sum.shape[0]
    rows, columns = queries.shape
    packed = pack_rows(queries, grad_out, attn_out, log_sum, qlen, ZS)
    packed, proj_weight = lax.optimization_barrier((packed, proj_weight))
    line = spread(packed, "psg", Z_GROUPS)
    near = jnp.stack([proj_weight] + [lax.ppermute(proj_weight, "psg", steps) for steps in X_STEPS])
    line, near = lax.optimization_barrier((line, near))
    gathered = spread(jnp.broadcast_to(line[None], (XS, *line.shape)), "psg", X_GROUPS)
    plus = lax.ppermute(near, "psg", z_step(-2))
    minus = lax.ppermute(near, "psg", z_step(2))
    far = lax.ppermute(near, "psg", z_step(4))
    above = lax.ppermute(jnp.concatenate([near, plus], axis=0), "psg", z_step(-1))
    below = lax.ppermute(jnp.concatenate([minus, near], axis=0), "psg", z_step(1))
    stripes = (near, plus, far, minus, above, below)
    question_total, top = attend.shape
    gathered = gathered.reshape(question_total, -1, rows, packed.shape[2])
    slots = min(question_total, 2 * question_total * top // (XS * ZS * CS))
    chosen, plan = select(attend, gathered, slots)
    chosen = spread(chosen, "psg", C_GROUPS)

    terms, grad_keys, grad_values = visits(plan, chosen, keys, values, heads)

    terms = spread(terms, "psg", C_GROUPS)
    pair = jnp.sum(terms.astype(jnp.float32), axis=0).astype(jnp.bfloat16)
    _, *stripes = lax.optimization_barrier((pair, *stripes))
    plane = spread(pair.reshape(XS * ZS, rows, columns), "psg", PLANE_GROUPS)
    own_weight = jnp.concatenate(stripes, axis=0)
    other_weight = lax.ppermute(own_weight, "psg", CORE_SWAP)
    grad_query = jnp.sum(plane.astype(jnp.float32), axis=0)

    parts = lax.axis_size("qry")
    terms = hidden_parts(grad_query, own_weight, other_weight, parts)
    terms = spread(terms, "qry", None)
    hidden = jnp.sum(terms.astype(jnp.float32), axis=0).astype(jnp.bfloat16)
    hidden = spread(jnp.broadcast_to(hidden[None], (parts, *hidden.shape)), "qry", None)
    grad_hidden = jnp.swapaxes(hidden.astype(jnp.float32), 0, 1).reshape(rows, -1)
    return (grad_query, grad_keys, grad_values, grad_hidden)


def solution(mesh):
    in_specs = (
        P("psg", "qry"),
        P("psg", "qry"),
        P("psg", "qry"),
        P("qry", "psg"),
        P("psg", "qry"),
        P("psg", "qry"),
        P("psg", "qry"),
        P(),
        P(),
    )
    out_specs = (P("psg", "qry"), P("psg", "qry"), P("psg", "qry"), P("psg", None))
    return jax.shard_map(
        on_device, mesh=mesh, in_specs=in_specs, out_specs=out_specs, check_vma=False
    )
```

```python
import functools

import jax
import jax.numpy as jnp
from jax import lax
from jax.experimental import pallas as pl
from jax.experimental.pallas import tpu as pltpu
from jax.sharding import PartitionSpec as P

WIDTH = 128
GROUP = 4
ASK_LEN = 256
XS, ZS, CS = 4, 8, 2
LOG2E = 1.4426950408889634
FAR = 1.0e6
WIDE = 63 * 2**20


def index_of(x, z, c):
    return (x * ZS + z) * CS + c


Z_GROUPS = [[index_of(x, z, c) for z in range(ZS)] for x in range(XS) for c in range(CS)]
X_GROUPS = [[index_of(x, z, c) for x in range(XS)] for z in range(ZS) for c in range(CS)]
C_GROUPS = [[index_of(x, z, c) for c in range(CS)] for x in range(XS) for z in range(ZS)]

PLANE_GROUPS = [[index_of(x, z, c) for x in range(XS) for z in range(ZS)] for c in range(CS)]

CORE_SWAP = [(i, i ^ 1) for i in range(XS * ZS * CS)]
X_STEPS = [
    [(index_of(x, z, c), index_of((x + k) % XS, z, c)) for x in range(XS) for z in range(ZS) for c in range(CS)]
    for k in range(1, XS)
]


def z_step(k):
    return [
        (index_of(x, z, c), index_of(x, (z + k) % ZS, c)) for x in range(XS) for z in range(ZS) for c in range(CS)
    ]


def spread(blocks, axis, groups):
    return lax.all_to_all(blocks, axis, 0, 0, tiled=True, axis_index_groups=groups)


def pack_kernel(heads, qlen_ref, query_in, grad_in, output_in, lse_in, out_ref, query_ref, grad_ref, output_ref, lse_ref, sems):
    copies = [
        pltpu.make_async_copy(source, target, sems.at[k])
        for k, (source, target) in enumerate(
            ((grad_in, grad_ref), (output_in, output_ref), (lse_in, lse_ref), (query_in, query_ref))
        )
    ]
    for copy in copies:
        copy.start()
    rows, columns = query_ref.shape
    shape = (rows, WIDTH)
    owner = lax.axis_index("psg")
    per_question = ASK_LEN // rows
    question = lax.div(owner, per_question)
    first = (owner - question * per_question) * rows
    column = lax.broadcasted_iota(jnp.int32, shape, 1)
    row = lax.broadcasted_iota(jnp.int32, shape, 0)
    live = first + row < qlen_ref[question]
    square = lax.broadcasted_iota(jnp.int32, (rows, rows), 0) == lax.broadcasted_iota(jnp.int32, (rows, rows), 1)
    value = jnp.zeros(shape, jnp.float32)
    for copy in copies:
        copy.wait()
    for head in range(heads):
        part = slice(head * WIDTH, (head + 1) * WIDTH)
        products = grad_ref[:, part].astype(jnp.float32) * output_ref[:, part].astype(jnp.float32)
        delta = jnp.sum(products, axis=1, keepdims=True)
        spread_lse = jnp.broadcast_to(lse_ref[head : head + 1, :], (rows, rows))
        shift = jnp.sum(jnp.where(square, spread_lse, 0.0), axis=1, keepdims=True) * (WIDTH**0.5)
        shift = jnp.where(live, shift, FAR)
        value = jnp.where(column % heads == head, jnp.where(column < 3 * heads, shift, delta), value)
    high = value.astype(jnp.bfloat16).astype(jnp.float32)
    middle = (value - high).astype(jnp.bfloat16).astype(jnp.float32)
    low = value - high - middle
    piece = (column // heads) % 3
    side = jnp.where(piece == 0, high, jnp.where(piece == 1, middle, low))
    side = jnp.where(column < 6 * heads, side, 0.0).astype(jnp.bfloat16)
    for copy in range(out_ref.shape[0]):
        out_ref[copy, :, :columns] = query_ref[...]
        out_ref[copy, :, columns : 2 * columns] = grad_ref[...]
        out_ref[copy, :, 2 * columns :] = side


def pack_rows(queries, grad_out, attn_out, log_sum, qlen, copies):
    rows, columns = queries.shape
    heads = log_sum.shape[0]
    anywhere = pl.BlockSpec(memory_space=pl.ANY)
    return pl.pallas_call(
        functools.partial(pack_kernel, heads),
        in_specs=[pl.BlockSpec(memory_space=pltpu.SMEM)] + [anywhere] * 4,
        out_specs=pl.BlockSpec(memory_space=pltpu.VMEM),
        out_shape=jax.ShapeDtypeStruct((copies, rows, 2 * columns + WIDTH), jnp.bfloat16),
        scratch_shapes=[
            pltpu.VMEM((rows, columns), jnp.bfloat16),
            pltpu.VMEM((rows, columns), jnp.bfloat16),
            pltpu.VMEM((rows, columns), jnp.bfloat16),
            pltpu.VMEM((heads, rows), jnp.float32),
            pltpu.SemaphoreType.DMA((4,)),
        ],
        compiler_params=pltpu.CompilerParams(vmem_limit_bytes=WIDE),
    )(qlen, queries, grad_out, attn_out, log_sum)


def select_kernel(attend_ref, rows_ref, out_ref, plan_ref):
    questions, top = attend_ref.shape
    slots = out_ref.shape[1]
    owner = lax.axis_index("psg")
    core = lax.rem(owner, CS)
    for target in range(CS):
        block = owner - core + target
        count = jnp.int32(0)
        chosen = [jnp.int32(0)] * slots
        for question in range(questions):
            hit = jnp.int32(0)
            for place in range(top):
                hit = hit | (attend_ref[question, place] == block).astype(jnp.int32)
            chosen = [jnp.where((hit == 1) & (count == k), question, chosen[k]) for k in range(slots)]
            count = count + hit

            @pl.when(core == target)
            def _():
                plan_ref[0, question] = hit
                plan_ref[1, question] = jnp.clip(count - 1, 0, slots - 1)

        for slot in range(slots):
            out_ref[target, slot] = rows_ref[chosen[slot]]


def select(attend, rows, slots):
    return pl.pallas_call(
        select_kernel,
        in_specs=[pl.BlockSpec(memory_space=pltpu.SMEM), pl.BlockSpec(memory_space=pltpu.VMEM)],
        out_specs=[pl.BlockSpec(memory_space=pltpu.VMEM), pl.BlockSpec(memory_space=pltpu.SMEM)],
        out_shape=[
            jax.ShapeDtypeStruct((CS, slots, *rows.shape[1:]), rows.dtype),
            jax.ShapeDtypeStruct((2, attend.shape[0]), jnp.int32),
        ],
        compiler_params=pltpu.CompilerParams(vmem_limit_bytes=16 * 2**20),
    )(attend, rows)


def visit_kernel(heads, plan, rows_ref, key_ref, value_ref, out_q, out_k, out_v):
    scale = WIDTH**-0.5
    span = key_ref.shape[0]
    cores, questions, chunks, chunk, _ = out_q.shape
    out_k[...] = jnp.zeros_like(out_k)
    out_v[...] = jnp.zeros_like(out_v)
    key_t = key_ref[...].astype(jnp.float32).T.astype(jnp.bfloat16)
    columns = lax.broadcasted_iota(jnp.int32, (span, WIDTH), 1)
    minus = []
    for head in range(heads):
        of_head = columns % heads == head
        for_shift = (columns < 3 * heads) & of_head
        for_delta = (columns >= 3 * heads) & (columns < 6 * heads) & of_head
        minus.append([jnp.where(here, -1.0, 0.0).astype(jnp.bfloat16) for here in (for_shift, for_delta)])

    @pl.loop(0, questions)
    def _(question):
        slot = plan[1, question]

        def take(start):
            return rows_ref[:, slot, :, :, start : start + WIDTH].reshape(ASK_LEN, WIDTH)

        @pl.when(plan[0, question] == 0)
        def _():
            out_q[:, question] = jnp.zeros((cores, chunks, chunk, heads * WIDTH), out_q.dtype)

        @pl.when(plan[0, question] != 0)
        def _():
            key = key_ref[...]
            value = value_ref[...]
            grad_k = jnp.zeros((span, WIDTH), jnp.float32)
            grad_v = jnp.zeros((span, WIDTH), jnp.float32)
            side = take(2 * heads * WIDTH)
            for head in range(heads):
                query = take(head * WIDTH)
                cotangent = take((heads + head) * WIDTH)
                minus_s, minus_d = minus[head]
                energy = lax.dot_general(
                    jnp.concatenate([key, minus_s], axis=1),
                    jnp.concatenate([query, side], axis=1),
                    (((1,), (1,)), ((), ())),
                    preferred_element_type=jnp.float32,
                )
                prob = jnp.exp2(energy * (scale * LOG2E))
                change = lax.dot_general(
                    jnp.concatenate([value, minus_d], axis=1),
                    jnp.concatenate([cotangent, side], axis=1),
                    (((1,), (1,)), ((), ())),
                    preferred_element_type=jnp.float32,
                )
                low_score = (prob * change).astype(jnp.bfloat16)
                low_prob = prob.astype(jnp.bfloat16)
                grad_k = grad_k + jnp.dot(low_score, query, preferred_element_type=jnp.float32)
                grad_v = grad_v + jnp.dot(low_prob, cotangent, preferred_element_type=jnp.float32)
                term = jnp.dot(key_t, low_score, preferred_element_type=jnp.float32).T * scale
                term = term.astype(jnp.bfloat16).reshape(cores, chunks, chunk, WIDTH)
                out_q[:, question, :, :, head * WIDTH : (head + 1) * WIDTH] = term
            out_k[...] += grad_k * scale
            out_v[...] += grad_v


def visits(plan, rows, keys, values, heads):
    cores, _, chunks, chunk, _ = rows.shape
    vmem = pl.BlockSpec(memory_space=pltpu.VMEM)
    return pl.pallas_call(
        functools.partial(visit_kernel, heads),
        in_specs=[pl.BlockSpec(memory_space=pltpu.SMEM), vmem, vmem, vmem],
        out_specs=[vmem, vmem, vmem],
        out_shape=[
            jax.ShapeDtypeStruct((cores, plan.shape[1], chunks, chunk, heads * WIDTH), jnp.bfloat16),
            jax.ShapeDtypeStruct(keys.shape, jnp.float32),
            jax.ShapeDtypeStruct(values.shape, jnp.float32),
        ],
        compiler_params=pltpu.CompilerParams(vmem_limit_bytes=32 * 2**20),
    )(plan, rows, keys, values)


def hidden_kernel(query_ref, own_ref, other_ref, out_ref):
    place = lax.axis_index("psg")
    core = lax.rem(place, CS)
    z = lax.rem(lax.div(place, CS), ZS)
    x = lax.div(place, CS * ZS)
    parts, _, wide = out_ref.shape
    depth = query_ref.shape[1]
    per_part = XS * ZS // parts

    def product(first_ref, second_ref):
        query = query_ref[...].astype(jnp.bfloat16)
        for part in range(parts):
            blocks = []
            for chip in range(part * per_part, (part + 1) * per_part):
                far_x = lax.rem(x - chip // ZS + XS, XS)
                off_z = lax.rem(chip % ZS - z + ZS, ZS)
                base = (lax.div(off_z, 2) + lax.rem(off_z, 2) * (ZS // 2)) * XS
                blocks += [first_ref[base + far_x], second_ref[base + far_x]]
            out_ref[part] = lax.dot_general(
                query,
                jnp.concatenate(blocks, axis=0).reshape(wide, depth),
                (((1,), (1,)), ((), ())),
                preferred_element_type=jnp.float32,
            ).astype(out_ref.dtype)

    @pl.when(core == 0)
    def _():
        product(own_ref, other_ref)

    @pl.when(core != 0)
    def _():
        product(other_ref, own_ref)


def hidden_parts(grad_query, own, other, parts):
    rows = grad_query.shape[0]
    wide = CS * own.shape[0] * own.shape[1] // parts
    vmem = pl.BlockSpec(memory_space=pltpu.VMEM)
    return pl.pallas_call(
        hidden_kernel,
        in_specs=[vmem, vmem, vmem],
        out_specs=vmem,
        out_shape=jax.ShapeDtypeStruct((parts, rows, wide), jnp.bfloat16),
        compiler_params=pltpu.CompilerParams(vmem_limit_bytes=16 * 2**20),
    )(grad_query, own, other)


def on_device(queries, grad_out, attn_out, log_sum, keys, values, proj_weight, attend, qlen):
    heads = log_sum.shape[0]
    rows, columns = queries.shape
    packed = pack_rows(queries, grad_out, attn_out, log_sum, qlen, ZS)
    packed, proj_weight = lax.optimization_barrier((packed, proj_weight))
    line = spread(packed, "psg", Z_GROUPS)
    near = jnp.stack([proj_weight] + [lax.ppermute(proj_weight, "psg", steps) for steps in X_STEPS])
    line, near = lax.optimization_barrier((line, near))
    gathered = spread(jnp.broadcast_to(line[None], (XS, *line.shape)), "psg", X_GROUPS)
    plus = lax.ppermute(near, "psg", z_step(-2))
    minus = lax.ppermute(near, "psg", z_step(2))
    far = lax.ppermute(near, "psg", z_step(4))
    above = lax.ppermute(jnp.concatenate([near, plus], axis=0), "psg", z_step(-1))
    below = lax.ppermute(jnp.concatenate([minus, near], axis=0), "psg", z_step(1))
    stripes = (near, plus, far, minus, above, below)
    question_total, top = attend.shape
    gathered = gathered.reshape(question_total, -1, rows, packed.shape[2])
    slots = min(question_total, 2 * question_total * top // (XS * ZS * CS))
    chosen, plan = select(attend, gathered, slots)
    chosen = spread(chosen, "psg", C_GROUPS)

    terms, grad_keys, grad_values = visits(plan, chosen, keys, values, heads)

    terms = spread(terms, "psg", C_GROUPS)
    pair = jnp.sum(terms.astype(jnp.float32), axis=0).astype(jnp.bfloat16)
    _, *stripes = lax.optimization_barrier((pair, *stripes))
    plane = spread(pair.reshape(XS * ZS, rows, columns), "psg", PLANE_GROUPS)
    own_weight = jnp.concatenate(stripes, axis=0)
    other_weight = lax.ppermute(own_weight, "psg", CORE_SWAP)
    grad_query = jnp.sum(plane.astype(jnp.float32), axis=0)

    parts = lax.axis_size("qry")
    terms = hidden_parts(grad_query, own_weight, other_weight, parts)
    terms = spread(terms, "qry", None)
    hidden = jnp.sum(terms.astype(jnp.float32), axis=0).astype(jnp.bfloat16)
    hidden = spread(jnp.broadcast_to(hidden[None], (parts, *hidden.shape)), "qry", None)
    grad_hidden = jnp.swapaxes(hidden.astype(jnp.float32), 0, 1).reshape(rows, -1)
    return (grad_query, grad_keys, grad_values, grad_hidden)


def solution(mesh):
    in_specs = (
        P("psg", "qry"),
        P("psg", "qry"),
        P("psg", "qry"),
        P("qry", "psg"),
        P("psg", "qry"),
        P("psg", "qry"),
        P("psg", "qry"),
        P(),
        P(),
    )
    out_specs = (P("psg", "qry"), P("psg", "qry"), P("psg", "qry"), P("psg", None))
    return jax.shard_map(
        on_device, mesh=mesh, in_specs=in_specs, out_specs=out_specs, check_vma=False
    )
```
